256 devices in a mesh: tm: 16 (over z_lo, y), space: 16 (over x, z_hi, core).
Axes of the slice: x: 4, y: 4, z: 8 (z_hi: 2, z_lo: 4; z = z_hi * 4 + z_lo), core: 2. Of those that a mesh axis runs over, the one named last changes fastest.
Arguments:
- starts: float32 [16, 2048, 2048], P('tm', 'space'), may hold values from -0.8 to 0.8
- stress: float32 [2, 2048, 2048], P(None, 'space'), may hold values from -5 to 5
Outputs:
- new_states: float32 [16, 2, 2048, 2048], P('tm', None, None, 'space')
The draws below stay inside these ranges and needn't reach their ends.
All inputs are finite; a program needn't handle non-finite values.
Results may differ from the reference program's by a relative error of at most 0.0003.
Values sent between devices are 32-bit elements; how exact they have to be, the bound alone decides.
A program may use at most 128 MiB of HBM per device.

```python
import jax
import jax.numpy as jnp

NG = 2048
KC = 512
FSTEPS = 1
SLICES = 16


def steps_of(key, dims, cuts, smallest, largest):
    gain = 1.0
    for axis_at, parts in cuts:
        heights = jax.random.uniform(jax.random.fold_in(jax.random.fold_in(key, 6), axis_at), (parts,), jnp.float32, smallest / len(cuts), largest / len(cuts))
        gain = gain * jnp.repeat(jnp.exp(heights), dims[axis_at] // parts).reshape((-1,) + (1,) * (len(dims) - 1 - axis_at))
    return gain


def normal_values(key, dims, scale, bound, shards=(), kind=jnp.bfloat16):
    values = scale * jax.random.normal(key, dims, jnp.float32)
    if shards:
        values = values * steps_of(key, dims, shards, -0.22, 0.18)
    return jnp.clip(values, -bound, bound).astype(kind)


def setup_inputs(seed: int = 0) -> dict:
    key_of = jax.random.split(jax.random.key(seed), 3)
    return {
        "starts": normal_values(key_of[0], (SLICES, NG, NG), 0.2, 0.8, ((0, 16), (1, 16)), jnp.float32),
        "stress": normal_values(key_of[1], (2, NG, NG), 1.0, 5.0, ((1, 16),), jnp.float32),
    }


step_size = 0.05
stiffness = 1.5
mean_mobility = 0.25


def wavenumbers(length):
    places = jnp.arange(length)
    signed = jnp.where(places < length // 2, places, places - length)
    waves = 2.0 * jnp.pi * signed.astype(jnp.float32) / length
    waves = jnp.where(places == length // 2, 0.0, waves).astype(jnp.float32)
    return waves, signed


def inverse(spectrum):
    return jnp.real(jnp.fft.ifft2(spectrum, norm="ortho"))


def fine_step(spectrum, stress, wave_rows, wave_cols, wave_square):
    height = 1.0 + inverse(spectrum)
    slope_rows = inverse(1j * wave_rows * spectrum)
    slope_cols = inverse(1j * wave_cols * spectrum)
    curve_rows = inverse(-1j * wave_rows * wave_square * spectrum)
    curve_cols = inverse(-1j * wave_cols * wave_square * spectrum)
    mobility = height ** 3 / 3.0
    marangoni = height * height / ((1.0 + height) ** 2)
    shear_factor = 0.5 * height * height
    flux_rows = mobility * curve_rows + marangoni * slope_rows + shear_factor * stress[0]
    flux_cols = mobility * curve_cols + marangoni * slope_cols + shear_factor * stress[1]
    forward_rows = jnp.fft.fft2(flux_rows, norm="ortho")
    forward_cols = jnp.fft.fft2(flux_cols, norm="ortho")
    diverge = 1j * wave_rows * forward_rows + 1j * wave_cols * forward_cols
    implicit = step_size * stiffness * wave_square * wave_square
    return (spectrum - step_size * diverge + implicit * spectrum) / (1.0 + implicit)


def reference(starts, stress):
    waves, freq_rows = wavenumbers(NG)
    wave_rows = waves[:, None]
    wave_cols = waves[None, :]
    wave_square = wave_rows * wave_rows + wave_cols * wave_cols
    window = jnp.abs(freq_rows) < KC // 2
    low_modes = (window[:, None] & window[None, :]).astype(jnp.float32)
    horizon = step_size * FSTEPS
    coarse_gain = 1.0 / (1.0 + horizon * (wave_square * wave_square / 3.0 - mean_mobility * wave_square))
    coarse = None
    outputs = []
    for member in range(SLICES):
        spectrum = jnp.fft.fft2(starts[member], norm="ortho")
        fine_state = spectrum
        for number in range(FSTEPS):
            fine_state = fine_step(fine_state, stress, wave_rows, wave_cols, wave_square)
        if member == 0:
            coarse = low_modes * spectrum
        coarse = coarse_gain * coarse + low_modes * (fine_state - coarse_gain * spectrum)
        result = (1.0 - low_modes) * fine_state + coarse
        outputs.append(jnp.stack([jnp.real(result), jnp.imag(result)]))
    return jnp.stack(outputs).astype(jnp.float32)
```

```python
import math

import jax
import jax.numpy as jnp
import ml_dtypes
import numpy as np
from jax import lax
from jax.experimental import pallas as pl
from jax.experimental.pallas import tpu as pltpu
from jax.sharding import PartitionSpec as P

NG = 2048
HALF = 1024
DT = 0.05
STIFF = 1.5
MEAN_MOBILITY = 0.25
MESH = pl.DeviceIdType.MESH
F32 = jnp.float32
BF16 = jnp.bfloat16


def split_np(values):
    hi = values.astype(np.float32).astype(ml_dtypes.bfloat16)
    lo = (values - hi.astype(np.float64)).astype(np.float32).astype(ml_dtypes.bfloat16)
    return hi, lo


def row_places():
    p = np.arange(128)
    return 16 * (p % 8) + p // 8


def forward_tables():
    y = np.arange(HALF)[:, None]
    tables = []
    for par in range(2):
        lane = np.arange(HALF)[None, :]
        block, slot, t = lane // 128, lane % 128 // 64, lane % 64
        ky = 128 * block + 2 * t + par
        angle = 2 * np.pi * ((ky * y) % NG) / NG
        table = np.where(slot == 0, np.cos(angle), -np.sin(angle))
        if par == 0:
            table[:, 64] = np.where(np.arange(HALF) % 2 == 0, 1.0, -1.0)
        tables.append(np.stack(split_np(table / math.sqrt(NG))))
    return np.stack(tables)


def derivative_table():
    k = np.arange(NG)
    wave = np.where(k < HALF, k, k - NG) * 2 * np.pi / NG
    wave[HALF] = 0.0
    local = row_places()
    target = local
    source = (128 * np.arange(16)[:, None] + local[None, :]).reshape(-1)
    gap = (target[:, None] - source[None, :]) % NG
    rows = [np.real(np.fft.ifft((1j * wave) ** m))[gap] for m in (1, 2, 3)]
    return np.concatenate(split_np(np.concatenate(rows)))


def column_tables():
    k1 = np.arange(128)[:, None]
    i = np.arange(128)[None, :]
    tables = []
    for q in range(16):
        angle = 2 * np.pi * ((q * k1 + 16 * i * k1) % NG) / NG
        c, s = np.cos(angle), np.sin(angle)
        table = np.block([[c, s], [-s, c]]) / math.sqrt(NG)
        tables.append(np.concatenate(split_np(table)))
    return np.stack(tables)


def lane_tables():
    tables = np.zeros((2, 256, 256))
    for par in range(2):
        for t in range(64):
            place = 2 * t + par
            mirrored = (128 - place) % 128
            for slot in range(2):
                source = par * 128 + slot * 64 + t
                tables[0, source, slot * 128 + place] = 1.0
                tables[1, source, slot * 128 + mirrored] = 1.0 - 2.0 * slot
    return tables.astype(ml_dtypes.bfloat16)


def reversal_table():
    table = np.zeros((128, 256))
    table[0, 128] = 1.0
    for k in range(1, 128):
        table[k, 128 - k] = 1.0
    return table.astype(ml_dtypes.bfloat16)


def order_table():
    table = np.zeros((128, 128))
    table[np.arange(128), row_places()] = 1.0
    return table.astype(ml_dtypes.bfloat16)


def split(values):
    hi = values.astype(BF16)
    return hi, (values - hi.astype(F32)).astype(BF16)


def dot(a, b):
    return jnp.dot(a, b, preferred_element_type=F32)


def dot_t(a, b):
    return lax.dot_general(a, b, (((1,), (1,)), ((), ())), preferred_element_type=F32)


def four(a, b, c, d):
    sr, si = a[0] + c[0], a[1] + c[1]
    dr, di = a[0] - c[0], a[1] - c[1]
    tr, ti = b[0] + d[0], b[1] + d[1]
    er, ei = b[0] - d[0], b[1] - d[1]
    return ((sr + tr, si + ti), (dr + ei, di - er), (sr - tr, si - ti), (dr - ei, di + er))


def turned(value, m):
    re, im = value
    if m == 0:
        return value
    if m == 4:
        return (im, -re)
    c, s = math.cos(2 * math.pi * m / 16), math.sin(2 * math.pi * m / 16)
    return (re * c + im * s, im * c - re * s)


def sixteen(values):
    stage = {}
    for q0 in range(4):
        parts = four(*[values[4 * q1 + q0] for q1 in range(4)])
        for ka in range(4):
            stage[ka, q0] = turned(parts[ka], q0 * ka)
    out = [None] * 16
    for ka in range(4):
        parts = four(*[stage[ka, q0] for q0 in range(4)])
        for kb in range(4):
            out[ka + 4 * kb] = parts[kb]
    return out


def waves_of(places):
    signed = jnp.where(places < HALF, places, places - NG)
    signed = jnp.where(places == HALF, 0, signed)
    return signed.astype(F32) * (2.0 * math.pi / NG)


def kernel(
    eta_ref, stress_ref, wf_hbm, d_hbm, l_hbm, p_ref, j_ref, q_ref, o_ref,
    wf, dm, lm, eta_in, stress_in, ep, sp, ub, sb1, xr, x2h, x2l, sb2, br,
    ib, fb, sb3, fr, zb, sbuf, slow, fin, ebuf, hr, er, dl, cr, co, cb,
    const_sem, p0_s, p0_r, s1, r1, s2, r2, s3, r3, so, ro, se, re_, sc, rc, sd, rd, ls,
):
    tm, space = lax.axis_index("tm"), lax.axis_index("space")
    zl, yp, h = tm // 4, tm % 4 // 2, tm % 2
    x, zh, c = space // 4, space // 2 % 2, space % 2
    par = x // 2
    block = (x + par * (3 - 2 * x)) * 4 + h * 2 + c
    my_r = x * 4 + h * 2 + c
    my_c = par * 8 + block
    my_slice = zl * 4 + 2 * yp + zh
    is_low = jnp.logical_and(h == 0, block < 2)

    def r_dev(s):
        return (zl * 4 + 2 * yp + s // 2 % 2, s // 4 * 4 + zh * 2 + s % 2)

    def c_dev(k):
        kp, kb = k // 8, k % 8
        xb = kb // 4
        xx = xb + kp * (3 - 2 * xb)
        return (zl * 4 + 2 * yp + kb // 2 % 2, xx * 4 + zh * 2 + kb % 2)

    def chain_dev(t):
        return (t // 4 * 4 + t % 4 // 2 * 2 + h, x * 4 + t % 2 * 2 + c)

    home_tm = zl * 4 + 2 * yp + zh

    def remote(src, dst, ss, rs, dev):
        return pltpu.make_async_remote_copy(
            src_ref=src, dst_ref=dst, send_sem=ss, recv_sem=rs, device_id=dev, device_id_type=MESH
        )

    barrier = pltpu.get_barrier_semaphore()

    def greet(n, carry):
        dev = (zl * 4 + 2 * yp + n // 16, n % 16)
        @pl.when(jnp.logical_or(dev[0] != tm, dev[1] != space))
        def _():
            pl.semaphore_signal(barrier, inc=1, device_id=dev, device_id_type=MESH)
        return carry

    lax.fori_loop(0, 32, greet, 0)

    def greet_chain(t, carry):
        @pl.when(t // 2 != zl * 2 + yp)
        def _():
            pl.semaphore_signal(barrier, inc=1, device_id=chain_dev(t), device_id_type=MESH)
        return carry

    lax.fori_loop(0, 16, greet_chain, 0)

    wf_copy = pltpu.make_async_copy(wf_hbm, wf, const_sem.at[0])
    d_copy = pltpu.make_async_copy(d_hbm, dm, const_sem.at[1])
    l_copy = pltpu.make_async_copy(l_hbm, lm, const_sem.at[2])
    wf_copy.start()
    d_copy.start()
    l_copy.start()
    pl.semaphore_wait(barrier, 45)

    lane = lax.broadcasted_iota(jnp.int32, (8, 128), 1)
    left = lane < 64
    t_lane = lane % 64
    sign = jnp.where(left, -1.0, 1.0)

    def half_turn(values):
        return pltpu.roll(values, 64, 1)

    def reorder(source, target):
        def body(n, carry):
            cols = pl.ds(pl.multiple_of(n * 256, 256), 256)
            values = source(cols)
            hi = values.astype(BF16)
            rest = values - hi.astype(F32)
            mid = rest.astype(BF16)
            last = (rest - mid.astype(F32)).astype(BF16)
            target[:, cols] = dot(q_ref[...], hi) + dot(q_ref[...], mid) + dot(q_ref[...], last)
            return carry

        lax.fori_loop(0, 8, body, 0)

    swaps = h != zh
    partner = (home_tm, x * 4 + h * 2 + c)
    eta_copy = remote(eta_ref.at[0], eta_in, p0_s.at[0], p0_r.at[0], partner)
    stress_copy = remote(stress_ref, stress_in, p0_s.at[1], p0_r.at[1], partner)

    @pl.when(swaps)
    def _():
        eta_copy.start()
        stress_copy.start()
        eta_copy.wait_recv()
        reorder(lambda cols: eta_in[:, cols], ep)

    @pl.when(jnp.logical_not(swaps))
    def _():
        reorder(lambda cols: eta_ref[0, :, cols], ep)

    def fold_start(n, carry):
        rows = pl.ds(pl.multiple_of(n * 16, 16), 16)
        lo_rows = pl.ds(pl.multiple_of(n * 16 + 128, 16), 16)
        first, second = ep[rows, :HALF], ep[rows, HALF:]
        for parity, values in ((0, first + second), (1, first - second)):
            hi, lo = split(values)
            ub[parity, rows, :] = hi
            ub[parity, lo_rows, :] = lo
        return carry

    lax.fori_loop(0, 8, fold_start, 0)
    wf_copy.wait()

    def begin(k, me, make, src, dst, sem):
        @pl.when(k != me)
        def _():
            make.start()

        @pl.when(k == me)
        def _():
            pltpu.make_async_copy(src, dst, sem).start()

    def t1_copy(k):
        return remote(sb1.at[k], xr.at[my_r], s1.at[k], r1.at[my_r], c_dev(k))

    def forward_start(n, carry):
        parity = n // 4
        cols = pl.ds(pl.multiple_of(n % 4 * 256, 256), 256)
        both = dot(ub[parity], wf[parity, 0, :, cols])
        out = both[:128] + both[128:] + dot(ub[parity, :128, :], wf[parity, 1, :, cols])
        for side in range(2):
            k = parity * 8 + n % 4 * 2 + side
            sb1[k] = out[:, side * 128 : side * 128 + 128].reshape(16, 8, 128)
            begin(k, my_c, t1_copy(k), sb1.at[k], xr.at[my_r], ls.at[0])
        return carry

    lax.fori_loop(0, 8, forward_start, 0)

    def wait_all(buffer, sems, me, sem, count, dev):
        def body(s, carry):
            @pl.when(s != me)
            def _():
                remote(buffer.at[s], buffer.at[s], sems.at[s], sems.at[s], dev).wait_recv()

            @pl.when(s == me)
            def _():
                pltpu.make_async_copy(buffer.at[s], buffer.at[s], sem).wait()

            return carry

        lax.fori_loop(0, count, body, 0)

    wait_all(xr, r1, my_r, ls.at[0], 16, partner)

    def spread(n, carry):
        own = xr[n % 16].reshape(128, 128)
        following = xr[(n + 1) % 16].reshape(128, 128)
        hi, lo = split(jnp.concatenate([own, following], axis=1))
        x2h[n] = hi
        x2l[n] = lo
        return carry

    lax.fori_loop(0, 32, spread, 0)
    d_copy.wait()

    def t2_copy(s):
        return remote(sb2.at[s], br.at[my_c], s2.at[s], r2.at[my_c], r_dev(s))

    def derive(n, carry):
        s = (my_r // 2 + n) % 8 * 2
        xh = x2h[pl.ds(s, 16)].reshape(NG, 256)
        xl = x2l[pl.ds(s, 16)].reshape(NG, 256)
        both = dot(dm[...], xh)
        out = both[:384] + both[384:] + dot(dm[:384, :], xl)
        for side in range(2):
            sb2[s + side] = out[:, side * 128 : side * 128 + 128]
            begin(s + side, my_r, t2_copy(s + side), sb2.at[s + side], br.at[my_c], ls.at[1])
        return carry

    lax.fori_loop(0, 8, derive, 0)

    @pl.when(swaps)
    def _():
        stress_copy.wait_recv()
        for f in range(2):
            reorder(lambda cols: stress_in[f, :, cols], sp.at[f])

    @pl.when(jnp.logical_not(swaps))
    def _():
        for f in range(2):
            reorder(lambda cols: stress_ref[f, :, cols], sp.at[f])

    wait_all(br, r2, my_c, ls.at[1], 16, partner)

    def column_waves(kb, kp, rows):
        lanes = lax.broadcasted_iota(jnp.int32, (rows, 128), 1) % 64
        return (128 * kb + 2 * lanes + kp).astype(F32) * (2.0 * math.pi / NG)

    def pack(k, carry):
        kp, kb = k // 8, k % 8
        ky = column_waves(kb, kp, 128)
        lanes = lax.broadcasted_iota(jnp.int32, (128, 128), 1)
        turn = jnp.where(lanes < 64, -ky, ky)
        weight = jnp.where(jnp.logical_and(k == 0, lanes % 64 == 0), 1.0, 2.0)
        x1, x2, x3 = br[k, 0:128, :], br[k, 128:256, :], br[k, 256:384, :]
        own = sb1[k].reshape(128, 128)
        cols = pl.ds(pl.multiple_of(kb * 128, 128), 128)
        fields = (
            x1,
            x3 - ky * ky * x1,
            half_turn(x2 - ky * ky * own) * turn,
            half_turn(own) * turn,
        )
        for f, values in enumerate(fields):
            hi, lo = split(values * weight)
            ib[kp, f * 128 : f * 128 + 128, cols] = hi
            ib[kp, 512 + f * 128 : 640 + f * 128, cols] = lo
        return carry

    lax.fori_loop(0, 16, pack, 0)

    def fluxes(n, carry):
        rows = pl.ds(pl.multiple_of(n * 256, 256), 256)
        sums = []
        for parity in range(2):
            both = dot_t(ib[parity], wf[parity, 0, rows, :])
            sums.append(both[:512] + both[512:] + dot_t(ib[parity, :512, :], wf[parity, 1, rows, :]))
        results = []
        for half in range(2):
            fields = sums[0] + sums[1] if half == 0 else sums[0] - sums[1]
            cols = pl.ds(pl.multiple_of(n * 256 + half * HALF, 256), 256)
            height = 1.0 + ep[:, cols]
            square = height * height
            mobility = square * height * (1.0 / 3.0)
            marangoni = square / ((1.0 + height) * (1.0 + height))
            shear = 0.5 * square
            results.append((
                mobility * fields[128:256] + marangoni * fields[0:128] + shear * sp[0, :, cols],
                mobility * fields[256:384] + marangoni * fields[384:512] + shear * sp[1, :, cols],
            ))
        for f in range(2):
            for parity in range(2):
                values = results[0][f] + results[1][f] if parity == 0 else results[0][f] - results[1][f]
                hi, lo = split(values)
                fb[parity, f * 128 : f * 128 + 128, rows] = hi
                fb[parity, 256 + f * 128 : 384 + f * 128, rows] = lo
        return carry

    lax.fori_loop(0, 4, fluxes, 0)

    def t3_copy(k):
        return remote(sb3.at[k], fr.at[my_r], s3.at[k], r3.at[my_r], c_dev(k))

    def forward_flux(n, carry):
        parity = n % 2
        cols = pl.ds(pl.multiple_of(n // 2 * 256, 256), 256)
        both = dot(fb[parity], wf[parity, 0, :, cols])
        out = both[:256] + both[256:] + dot(fb[parity, :256, :], wf[parity, 1, :, cols])
        for side in range(2):
            k = parity * 8 + n // 2 * 2 + side
            sb3[k] = out[:, side * 128 : side * 128 + 128].reshape(2, 16, 8, 128)
            begin(k, my_c, t3_copy(k), sb3.at[k], fr.at[my_r], ls.at[2])
        return carry

    lax.fori_loop(0, 8, forward_flux, 0)
    l_copy.wait()

    def column_pass(pair):
        def body(q, carry):
            hi, lo = split(jnp.concatenate(pair(q), axis=0))
            both = dot(lm[q], hi)
            zb[q] = both[:256] + both[256:] + dot(lm[q, :256, :], lo)
            return carry

        lax.fori_loop(0, 16, body, 0)

    def sixteen_at(kt):
        rows = pl.ds(pl.multiple_of(kt * 8, 8), 8)
        im_rows = pl.ds(pl.multiple_of(128 + kt * 8, 8), 8)
        return rows, sixteen([(zb[q, rows, :], zb[q, im_rows, :]) for q in range(16)])

    def start_pair(q):
        values = xr[:, q].reshape(128, 128)
        return [values, half_turn(values)]

    column_pass(start_pair)

    def start_rows(kt, carry):
        rows, out = sixteen_at(kt)
        for k0 in range(16):
            sbuf[k0, rows, :] = jnp.where(left, out[k0][0], half_turn(out[k0][1]))
        return carry

    lax.fori_loop(0, 16, start_rows, 0)

    def reversed_rows(buffer, k0):
        hi, lo = split(jnp.concatenate([buffer[15 - k0], buffer[(16 - k0) % 16]], axis=0))
        return dot(j_ref[...], hi) + dot(j_ref[...], lo)

    lanes128 = lax.broadcasted_iota(jnp.int32, (128, 128), 1)
    at_first = lanes128 % 64 == 0
    conj_sign = jnp.where(lanes128 < 64, 1.0, -1.0)
    has_pack = jnp.logical_and(par == 0, block == 0)

    def keep_low(ci, carry):
        slow[ci] = sbuf[ci + ci // 2 * 12]
        return carry

    lax.fori_loop(0, 4, keep_low, 0)

    @pl.when(has_pack)
    def _():
        def body(ci, carry):
            k0 = ci + ci // 2 * 12
            mirrored = reversed_rows(sbuf, k0) * conj_sign
            slow[ci] = jnp.where(at_first, 0.5 * (sbuf[k0] + mirrored), sbuf[k0])
            return carry

        lax.fori_loop(0, 4, body, 0)

    wait_all(fr, r3, my_r, ls.at[2], 16, partner)
    ky128 = column_waves(block, par, 128)
    turn128 = jnp.where(lanes128 < 64, -ky128, ky128)

    def flux_pair(q):
        first = fr[:, 0, q].reshape(128, 128)
        second = half_turn(fr[:, 1, q].reshape(128, 128)) * turn128
        return [
            jnp.where(lanes128 < 64, first, half_turn(second)),
            jnp.where(lanes128 < 64, half_turn(first), second),
        ]

    column_pass(flux_pair)
    ky8 = column_waves(block, par, 8)

    def flux_rows(kt, carry):
        rows, out = sixteen_at(kt)
        for k0 in range(16):
            places = 128 * k0 + kt * 8 + lax.broadcasted_iota(jnp.int32, (8, 128), 0)
            kx = waves_of(places)
            square = kx * kx + ky8 * ky8
            scale = DT / (1.0 + (DT * STIFF) * square * square)
            diverge = half_turn(out[k0][0]) * jnp.where(left, 1.0, kx) + out[k0][1] * jnp.where(left, -kx, 1.0)
            fin[k0, rows, :] = sbuf[k0, rows, :] - scale * diverge
        return carry

    lax.fori_loop(0, 16, flux_rows, 0)

    @pl.when(has_pack)
    def _():
        def body(k0, carry):
            mirrored = reversed_rows(fin, k0) * conj_sign
            zb[k0, 0:128, :] = jnp.where(at_first, 0.5 * (fin[k0] + mirrored), fin[k0])
            zb[k0, 128:256, :] = half_turn(fin[k0] - mirrored) * (0.5 * conj_sign)
            return carry

        lax.fori_loop(0, 16, body, 0)

        def back(k0, carry):
            fin[k0] = zb[k0, 0:128, :]
            return carry

        lax.fori_loop(0, 16, back, 0)

    home_b = (home_tm, block)
    home_m = (home_tm, 15 - block)
    same_home = jnp.logical_and(home_tm == tm, block == space)
    spans = ((2, 12), (0, 2), (14, 2))

    def out_copies(n):
        first, count = spans[n]
        src = fin.at[pl.ds(first, count)]
        dst = hr.at[par, pl.ds(first, count)]
        return (
            remote(src, dst, so.at[n], ro.at[par, n], home_b),
            remote(src, dst, so.at[3 + n], ro.at[par, n], home_m),
            pltpu.make_async_copy(src, dst, ls.at[3 + n]),
        )

    def begin_out(n):
        direct, mirror, local = out_copies(n)
        mirror.start()

        @pl.when(same_home)
        def _():
            local.start()

        @pl.when(jnp.logical_not(same_home))
        def _():
            direct.start()

    begin_out(0)
    def low_block(t):
        ci = t // 4
        return ci, ci + ci // 2 * 12, pl.multiple_of(t % 4 * 32, 32)

    def low_tables(t):
        ci, k0, first = low_block(t)
        places = 128 * k0 + first + lax.broadcasted_iota(jnp.int32, (32, 128), 0)
        kx = waves_of(places)
        ky = column_waves(block, par, 32)
        square = kx * kx + ky * ky
        gain = 1.0 / (1.0 + DT * (square * square * (1.0 / 3.0) - MEAN_MOBILITY * square))
        return gain, places != NG - 256

    def chain_out(t):
        return remote(dl.at[t], cr.at[my_slice], sc.at[t], rc.at[my_slice], chain_dev(t))

    def chain_back(t):
        return remote(co.at[t], cb.at[my_slice], sd.at[t], rd.at[my_slice], chain_dev(t))

    @pl.when(is_low)
    def _():
        def defects(t, carry):
            ci, k0, first = low_block(t)
            gain, keep = low_tables(t)
            gain = jnp.where(my_slice == 0, 0.0, gain)
            rows = pl.ds(first, 32)
            dl[t] = jnp.where(keep, fin[k0, rows, :] - gain * slow[ci, rows, :], 0.0)
            begin(t, my_slice, chain_out(t), dl.at[t], cr.at[my_slice], ls.at[6])
            return carry

        lax.fori_loop(0, 16, defects, 0)
        wait_all(cr, rc, my_slice, ls.at[6], 16, partner)
        gain, keep = low_tables(my_slice)

        def advance(t, current):
            current = gain * current + cr[t]
            co[t] = current
            begin(t, my_slice, chain_back(t), co.at[t], cb.at[my_slice], ls.at[7])
            return current

        lax.fori_loop(0, 16, advance, jnp.zeros((32, 128), F32))
        wait_all(cb, rd, my_slice, ls.at[7], 16, partner)

        def merge(t, carry):
            ci, k0, first = low_block(t)
            gain, keep = low_tables(t)
            rows = pl.ds(first, 32)
            fin[k0, rows, :] = jnp.where(keep, cb[t], fin[k0, rows, :])
            return carry

        lax.fori_loop(0, 16, merge, 0)

    begin_out(1)
    begin_out(2)
    extra_home = jnp.where(block == 0, 8, 16 - block)
    extra_copy = remote(ebuf, er, se.at[0], re_.at[0], (home_tm, extra_home))

    @pl.when(par == 0)
    def _():
        def body(k0, carry):
            tile = jnp.transpose(jnp.where(has_pack, zb[k0, 128:256, :], fin[k0]))
            ebuf[k0, 0:1, :] = tile[0:1, :]
            ebuf[k0, 1:2, :] = tile[64:65, :]
            return carry

        lax.fori_loop(0, 16, body, 0)
        extra_copy.start()


    is_mirror = space >= 8
    for source_par in range(2):
        local_here = jnp.logical_and(same_home, par == source_par)
        for n in range(3):
            first, count = spans[n]
            view = hr.at[source_par, pl.ds(first, count)]

            @pl.when(local_here)
            def _():
                pltpu.make_async_copy(view, view, ls.at[3 + n]).wait()

            @pl.when(jnp.logical_not(local_here))
            def _():
                remote(view, view, ro.at[source_par, n], ro.at[source_par, n], partner).wait_recv()

    @pl.when(is_mirror)
    def _():
        remote(er, er, re_.at[0], re_.at[0], partner).wait_recv()

        def body(k0, carry):
            rows = lax.broadcasted_iota(jnp.int32, (128, 128), 0)
            tile = jnp.where(rows == 0, er[k0, 0:1, :], jnp.where(rows == 64, er[k0, 1:2, :], 0.0))
            hr[0, k0] = jnp.where(at_first, jnp.transpose(tile), hr[0, k0])
            return carry

        lax.fori_loop(0, 16, body, 0)

    def ordered(k0, table):
        hi, lo = split(jnp.concatenate([hr[0, k0], hr[1, k0]], axis=1))
        return dot(hi, table) + dot(lo, table)

    def put(k0, values):
        rows = pl.ds(pl.multiple_of(k0 * 128, 128), 128)
        o_ref[0, 0, rows, :] = values[:, :128]
        o_ref[0, 1, rows, :] = values[:, 128:]

    @pl.when(jnp.logical_not(is_mirror))
    def _():
        def body(k0, carry):
            put(k0, ordered(k0, p_ref[0]))
            return carry

        lax.fori_loop(0, 16, body, 0)

    @pl.when(is_mirror)
    def _():
        def body(k0, carry):
            values = ordered(k0, p_ref[1])
            zb[k0, 0:128, :] = values[:, :128]
            zb[k0, 128:256, :] = values[:, 128:]
            return carry

        lax.fori_loop(0, 16, body, 0)

        def turn_rows(k0, carry):
            one, two = 15 - k0, (16 - k0) % 16
            upper = jnp.concatenate([zb[one, 0:128, :], zb[one, 128:256, :]], axis=1)
            lower = jnp.concatenate([zb[two, 0:128, :], zb[two, 128:256, :]], axis=1)
            hi, lo = split(jnp.concatenate([upper, lower], axis=0))
            put(k0, dot(j_ref[...], hi) + dot(j_ref[...], lo))
            return carry

        lax.fori_loop(0, 16, turn_rows, 0)

    @pl.when(swaps)
    def _():
        eta_copy.wait_send()
        stress_copy.wait_send()

    def sent(k, carry):
        @pl.when(k != my_c)
        def _():
            t1_copy(k).wait_send()
            t3_copy(k).wait_send()

        @pl.when(k != my_r)
        def _():
            t2_copy(k).wait_send()

        return carry

    lax.fori_loop(0, 16, sent, 0)
    for n in range(3):
        direct, mirror, local = out_copies(n)
        mirror.wait_send()

        @pl.when(jnp.logical_not(same_home))
        def _():
            direct.wait_send()

    @pl.when(par == 0)
    def _():
        extra_copy.wait_send()

    @pl.when(is_low)
    def _():
        def body(t, carry):
            @pl.when(t != my_slice)
            def _():
                chain_out(t).wait_send()
                chain_back(t).wait_send()

            return carry

        lax.fori_loop(0, 16, body, 0)


def solution(mesh):
    tables = [
        forward_tables(),
        derivative_table(),
        column_tables(),
        lane_tables(),
        reversal_table(),
        order_table(),
    ]
    vmem = pl.BlockSpec(memory_space=pltpu.VMEM)
    anywhere = pl.BlockSpec(memory_space=pl.ANY)
    dma = pltpu.SemaphoreType.DMA

    def shards(starts, stress):
        return pl.pallas_call(
            kernel,
            out_shape=jax.ShapeDtypeStruct((1, 2, NG, 128), F32),
            in_specs=[vmem, vmem, anywhere, anywhere, anywhere, vmem, vmem, vmem],
            out_specs=vmem,
            scratch_shapes=[
                pltpu.VMEM((2, 2, HALF, HALF), BF16),
                pltpu.VMEM((768, NG), BF16),
                pltpu.VMEM((16, 512, 256), BF16),
                pltpu.VMEM((128, NG), F32),
                pltpu.VMEM((2, 128, NG), F32),
                pltpu.VMEM((128, NG), F32),
                pltpu.VMEM((2, 128, NG), F32),
                pltpu.VMEM((2, 256, HALF), BF16),
                pltpu.VMEM((16, 16, 8, 128), F32),
                pltpu.VMEM((16, 16, 8, 128), F32),
                pltpu.VMEM((32, 128, 256), BF16),
                pltpu.VMEM((32, 128, 256), BF16),
                pltpu.VMEM((16, 384, 128), F32),
                pltpu.VMEM((16, 384, 128), F32),
                pltpu.VMEM((2, 1024, HALF), BF16),
                pltpu.VMEM((2, 512, HALF), BF16),
                pltpu.VMEM((16, 2, 16, 8, 128), F32),
                pltpu.VMEM((16, 2, 16, 8, 128), F32),
                pltpu.VMEM((16, 256, 128), F32),
                pltpu.VMEM((16, 128, 128), F32),
                pltpu.VMEM((4, 128, 128), F32),
                pltpu.VMEM((16, 128, 128), F32),
                pltpu.VMEM((16, 8, 128), F32),
                pltpu.VMEM((2, 16, 128, 128), F32),
                pltpu.VMEM((16, 8, 128), F32),
                pltpu.VMEM((16, 32, 128), F32),
                pltpu.VMEM((16, 32, 128), F32),
                pltpu.VMEM((16, 32, 128), F32),
                pltpu.VMEM((16, 32, 128), F32),
                dma((3,)), dma((2,)), dma((2,)),
                dma((16,)), dma((16,)), dma((16,)), dma((16,)), dma((16,)), dma((16,)),
                dma((6,)), dma((2, 3)), dma((1,)), dma((1,)),
                dma((16,)), dma((16,)), dma((16,)), dma((16,)), dma((8,)),
            ],
            compiler_params=pltpu.CompilerParams(
                collective_id=0, has_side_effects=True, vmem_limit_bytes=62 * 1024 * 1024
            ),
            name="parareal",
        )(starts, stress, *[jnp.asarray(table) for table in tables])

    return jax.shard_map(
        shards,
        mesh=mesh,
        in_specs=(P("tm", "space", None), P(None, "space", None)),
        out_specs=P("tm", None, None, "space"),
        check_vma=False,
    )
```

```python
import math

import jax
import jax.numpy as jnp
import ml_dtypes
import numpy as np
from jax import lax
from jax.experimental import pallas as pl
from jax.experimental.pallas import tpu as pltpu
from jax.sharding import PartitionSpec as P

NG = 2048
HALF = 1024
DT = 0.05
STIFF = 1.5
MEAN_MOBILITY = 0.25
MESH = pl.DeviceIdType.MESH
F32 = jnp.float32
BF16 = jnp.bfloat16


def split_np(values):
    hi = values.astype(np.float32).astype(ml_dtypes.bfloat16)
    lo = (values - hi.astype(np.float64)).astype(np.float32).astype(ml_dtypes.bfloat16)
    return hi, lo


def row_places():
    p = np.arange(128)
    return 16 * (p % 8) + p // 8


def forward_tables():
    y = np.arange(HALF)[:, None]
    tables = []
    for par in range(2):
        lane = np.arange(HALF)[None, :]
        block, slot, t = lane // 128, lane % 128 // 64, lane % 64
        ky = 128 * block + 2 * t + par
        angle = 2 * np.pi * ((ky * y) % NG) / NG
        table = np.where(slot == 0, np.cos(angle), -np.sin(angle))
        if par == 0:
            table[:, 64] = np.where(np.arange(HALF) % 2 == 0, 1.0, -1.0)
        tables.append(np.stack(split_np(table / math.sqrt(NG))))
    return np.stack(tables)


def derivative_table():
    k = np.arange(NG)
    wave = np.where(k < HALF, k, k - NG) * 2 * np.pi / NG
    wave[HALF] = 0.0
    local = row_places()
    target = local
    source = (128 * np.arange(16)[:, None] + local[None, :]).reshape(-1)
    gap = (target[:, None] - source[None, :]) % NG
    rows = [np.real(np.fft.ifft((1j * wave) ** m))[gap] for m in (1, 2, 3)]
    return np.concatenate(split_np(np.concatenate(rows)))


def column_tables():
    k1 = np.arange(128)[:, None]
    i = np.arange(128)[None, :]
    tables = []
    for q in range(16):
        angle = 2 * np.pi * ((q * k1 + 16 * i * k1) % NG) / NG
        c, s = np.cos(angle), np.sin(angle)
        table = np.block([[c, s], [-s, c]]) / math.sqrt(NG)
        tables.append(np.concatenate(split_np(table)))
    return np.stack(tables)


def lane_tables():
    tables = np.zeros((2, 256, 256))
    for par in range(2):
        for t in range(64):
            place = 2 * t + par
            mirrored = (128 - place) % 128
            for slot in range(2):
                source = par * 128 + slot * 64 + t
                tables[0, source, slot * 128 + place] = 1.0
                tables[1, source, slot * 128 + mirrored] = 1.0 - 2.0 * slot
    return tables.astype(ml_dtypes.bfloat16)


def reversal_table():
    table = np.zeros((128, 256))
    table[0, 128] = 1.0
    for k in range(1, 128):
        table[k, 128 - k] = 1.0
    return table.astype(ml_dtypes.bfloat16)


def order_table():
    table = np.zeros((128, 128))
    table[np.arange(128), row_places()] = 1.0
    return table.astype(ml_dtypes.bfloat16)


def split(values):
    hi = values.astype(BF16)
    return hi, (values - hi.astype(F32)).astype(BF16)


def dot(a, b):
    return jnp.dot(a, b, preferred_element_type=F32)


def dot_t(a, b):
    return lax.dot_general(a, b, (((1,), (1,)), ((), ())), preferred_element_type=F32)


def four(a, b, c, d):
    sr, si = a[0] + c[0], a[1] + c[1]
    dr, di = a[0] - c[0], a[1] - c[1]
    tr, ti = b[0] + d[0], b[1] + d[1]
    er, ei = b[0] - d[0], b[1] - d[1]
    return ((sr + tr, si + ti), (dr + ei, di - er), (sr - tr, si - ti), (dr - ei, di + er))


def turned(value, m):
    re, im = value
    if m == 0:
        return value
    if m == 4:
        return (im, -re)
    c, s = math.cos(2 * math.pi * m / 16), math.sin(2 * math.pi * m / 16)
    return (re * c + im * s, im * c - re * s)


def sixteen(values):
    stage = {}
    for q0 in range(4):
        parts = four(*[values[4 * q1 + q0] for q1 in range(4)])
        for ka in range(4):
            stage[ka, q0] = turned(parts[ka], q0 * ka)
    out = [None] * 16
    for ka in range(4):
        parts = four(*[stage[ka, q0] for q0 in range(4)])
        for kb in range(4):
            out[ka + 4 * kb] = parts[kb]
    return out


def waves_of(places):
    signed = jnp.where(places < HALF, places, places - NG)
    signed = jnp.where(places == HALF, 0, signed)
    return signed.astype(F32) * (2.0 * math.pi / NG)


def kernel(
    eta_ref, stress_ref, wf_hbm, d_hbm, l_hbm, p_ref, j_ref, q_ref, o_ref,
    wf, dm, lm, ep, sp, ub, sb1, xr, x2h, x2l, sb2, br,
    ib, fb, sb3, fr, zb, sbuf, slow, fin, ebuf, hr, er, dl, cr, co, cb,
    const_sem, s1, r1, s2, r2, s3, r3, so, ro, se, re_, sc, rc, sd, rd, ls,
):
    tm, space = lax.axis_index("tm"), lax.axis_index("space")
    x, zh, c = space // 4, space // 2 % 2, space % 2
    par = x // 2
    block = (x + par * (3 - 2 * x)) * 4 + zh * 2 + c
    my_r = space
    my_c = par * 8 + block
    my_slice = tm
    is_low = jnp.logical_and(zh == 0, block < 2)
    partner = (tm, (space + 1) % 16)

    def r_dev(s):
        return (tm, s)

    def c_dev(k):
        kp, kb = k // 8, k % 8
        xb = kb // 4
        return (tm, (xb + kp * (3 - 2 * xb)) * 4 + kb % 4)

    def chain_dev(t):
        return (t, space)

    def remote(src, dst, ss, rs, dev):
        return pltpu.make_async_remote_copy(
            src_ref=src, dst_ref=dst, send_sem=ss, recv_sem=rs, device_id=dev, device_id_type=MESH
        )

    barrier = pltpu.get_barrier_semaphore()

    def greet(n, carry):
        pl.semaphore_signal(barrier, inc=1, device_id=(tm, (space + n) % 16), device_id_type=MESH)
        pl.semaphore_signal(barrier, inc=1, device_id=((tm + n) % 16, space), device_id_type=MESH)
        return carry

    lax.fori_loop(1, 16, greet, 0)

    wf_copy = pltpu.make_async_copy(wf_hbm, wf, const_sem.at[0])
    d_copy = pltpu.make_async_copy(d_hbm, dm, const_sem.at[1])
    l_copy = pltpu.make_async_copy(l_hbm, lm, const_sem.at[2])
    wf_copy.start()
    d_copy.start()
    l_copy.start()
    pl.semaphore_wait(barrier, 30)

    lane = lax.broadcasted_iota(jnp.int32, (8, 128), 1)
    left = lane < 64
    t_lane = lane % 64
    sign = jnp.where(left, -1.0, 1.0)

    def half_turn(values):
        return pltpu.roll(values, 64, 1)

    def reorder(source, target):
        def body(n, carry):
            cols = pl.ds(pl.multiple_of(n * 256, 256), 256)
            values = source(cols)
            hi = values.astype(BF16)
            rest = values - hi.astype(F32)
            mid = rest.astype(BF16)
            last = (rest - mid.astype(F32)).astype(BF16)
            target[:, cols] = dot(q_ref[...], hi) + dot(q_ref[...], mid) + dot(q_ref[...], last)
            return carry

        lax.fori_loop(0, 8, body, 0)

    reorder(lambda cols: eta_ref[0, :, cols], ep)

    def fold_start(n, carry):
        rows = pl.ds(pl.multiple_of(n * 16, 16), 16)
        lo_rows = pl.ds(pl.multiple_of(n * 16 + 128, 16), 16)
        first, second = ep[rows, :HALF], ep[rows, HALF:]
        for parity, values in ((0, first + second), (1, first - second)):
            hi, lo = split(values)
            ub[parity, rows, :] = hi
            ub[parity, lo_rows, :] = lo
        return carry

    lax.fori_loop(0, 8, fold_start, 0)
    wf_copy.wait()

    def begin(k, me, make, src, dst, sem):
        @pl.when(k != me)
        def _():
            make.start()

        @pl.when(k == me)
        def _():
            pltpu.make_async_copy(src, dst, sem).start()

    def t1_copy(k):
        return remote(sb1.at[k], xr.at[my_r], s1.at[k], r1.at[my_r], c_dev(k))

    def forward_start(n, carry):
        parity = n // 4
        cols = pl.ds(pl.multiple_of(n % 4 * 256, 256), 256)
        both = dot(ub[parity], wf[parity, 0, :, cols])
        out = both[:128] + both[128:] + dot(ub[parity, :128, :], wf[parity, 1, :, cols])
        for side in range(2):
            k = parity * 8 + n % 4 * 2 + side
            sb1[k] = out[:, side * 128 : side * 128 + 128].reshape(16, 8, 128)
            begin(k, my_c, t1_copy(k), sb1.at[k], xr.at[my_r], ls.at[0])
        return carry

    lax.fori_loop(0, 8, forward_start, 0)

    def wait_all(buffer, sems, me, sem, count, dev):
        def body(s, carry):
            @pl.when(s != me)
            def _():
                remote(buffer.at[s], buffer.at[s], sems.at[s], sems.at[s], dev).wait_recv()

            @pl.when(s == me)
            def _():
                pltpu.make_async_copy(buffer.at[s], buffer.at[s], sem).wait()

            return carry

        lax.fori_loop(0, count, body, 0)

    wait_all(xr, r1, my_r, ls.at[0], 16, partner)

    def spread(n, carry):
        own = xr[n % 16].reshape(128, 128)
        following = xr[(n + 1) % 16].reshape(128, 128)
        hi, lo = split(jnp.concatenate([own, following], axis=1))
        x2h[n] = hi
        x2l[n] = lo
        return carry

    lax.fori_loop(0, 32, spread, 0)
    d_copy.wait()

    def t2_copy(s):
        return remote(sb2.at[s], br.at[my_c], s2.at[s], r2.at[my_c], r_dev(s))

    def derive(n, carry):
        s = (my_r // 2 + n) % 8 * 2
        xh = x2h[pl.ds(s, 16)].reshape(NG, 256)
        xl = x2l[pl.ds(s, 16)].reshape(NG, 256)
        both = dot(dm[...], xh)
        out = both[:384] + both[384:] + dot(dm[:384, :], xl)
        for side in range(2):
            sb2[s + side] = out[:, side * 128 : side * 128 + 128]
            begin(s + side, my_r, t2_copy(s + side), sb2.at[s + side], br.at[my_c], ls.at[1])
        return carry

    lax.fori_loop(0, 8, derive, 0)

    for f in range(2):
        reorder(lambda cols: stress_ref[f, :, cols], sp.at[f])

    wait_all(br, r2, my_c, ls.at[1], 16, partner)

    def column_waves(kb, kp, rows):
        lanes = lax.broadcasted_iota(jnp.int32, (rows, 128), 1) % 64
        return (128 * kb + 2 * lanes + kp).astype(F32) * (2.0 * math.pi / NG)

    def pack(k, carry):
        kp, kb = k // 8, k % 8
        ky = column_waves(kb, kp, 128)
        lanes = lax.broadcasted_iota(jnp.int32, (128, 128), 1)
        turn = jnp.where(lanes < 64, -ky, ky)
        weight = jnp.where(jnp.logical_and(k == 0, lanes % 64 == 0), 1.0, 2.0)
        x1, x2, x3 = br[k, 0:128, :], br[k, 128:256, :], br[k, 256:384, :]
        own = sb1[k].reshape(128, 128)
        cols = pl.ds(pl.multiple_of(kb * 128, 128), 128)
        fields = (
            x1,
            x3 - ky * ky * x1,
            half_turn(x2 - ky * ky * own) * turn,
            half_turn(own) * turn,
        )
        for f, values in enumerate(fields):
            hi, lo = split(values * weight)
            ib[kp, f * 128 : f * 128 + 128, cols] = hi
            ib[kp, 512 + f * 128 : 640 + f * 128, cols] = lo
        return carry

    lax.fori_loop(0, 16, pack, 0)

    def fluxes(n, carry):
        rows = pl.ds(pl.multiple_of(n * 256, 256), 256)
        sums = []
        for parity in range(2):
            both = dot_t(ib[parity], wf[parity, 0, rows, :])
            sums.append(both[:512] + both[512:] + dot_t(ib[parity, :512, :], wf[parity, 1, rows, :]))
        results = []
        for half in range(2):
            fields = sums[0] + sums[1] if half == 0 else sums[0] - sums[1]
            cols = pl.ds(pl.multiple_of(n * 256 + half * HALF, 256), 256)
            height = 1.0 + ep[:, cols]
            square = height * height
            mobility = square * height * (1.0 / 3.0)
            marangoni = square / ((1.0 + height) * (1.0 + height))
            shear = 0.5 * square
            results.append((
                mobility * fields[128:256] + marangoni * fields[0:128] + shear * sp[0, :, cols],
                mobility * fields[256:384] + marangoni * fields[384:512] + shear * sp[1, :, cols],
            ))
        for f in range(2):
            for parity in range(2):
                values = results[0][f] + results[1][f] if parity == 0 else results[0][f] - results[1][f]
                hi, lo = split(values)
                fb[parity, f * 128 : f * 128 + 128, rows] = hi
                fb[parity, 256 + f * 128 : 384 + f * 128, rows] = lo
        return carry

    lax.fori_loop(0, 4, fluxes, 0)

    def t3_copy(k):
        return remote(sb3.at[k], fr.at[my_r], s3.at[k], r3.at[my_r], c_dev(k))

    def forward_flux(n, carry):
        parity = n % 2
        cols = pl.ds(pl.multiple_of(n // 2 * 256, 256), 256)
        both = dot(fb[parity], wf[parity, 0, :, cols])
        out = both[:256] + both[256:] + dot(fb[parity, :256, :], wf[parity, 1, :, cols])
        for side in range(2):
            k = parity * 8 + n // 2 * 2 + side
            sb3[k] = out[:, side * 128 : side * 128 + 128].reshape(2, 16, 8, 128)
            begin(k, my_c, t3_copy(k), sb3.at[k], fr.at[my_r], ls.at[2])
        return carry

    lax.fori_loop(0, 8, forward_flux, 0)
    l_copy.wait()

    def column_pass(pair):
        def body(q, carry):
            hi, lo = split(jnp.concatenate(pair(q), axis=0))
            both = dot(lm[q], hi)
            zb[q] = both[:256] + both[256:] + dot(lm[q, :256, :], lo)
            return carry

        lax.fori_loop(0, 16, body, 0)

    def sixteen_at(kt):
        rows = pl.ds(pl.multiple_of(kt * 8, 8), 8)
        im_rows = pl.ds(pl.multiple_of(128 + kt * 8, 8), 8)
        return rows, sixteen([(zb[q, rows, :], zb[q, im_rows, :]) for q in range(16)])

    def start_pair(q):
        values = xr[:, q].reshape(128, 128)
        return [values, half_turn(values)]

    column_pass(start_pair)

    def start_rows(kt, carry):
        rows, out = sixteen_at(kt)
        for k0 in range(16):
            sbuf[k0, rows, :] = jnp.where(left, out[k0][0], half_turn(out[k0][1]))
        return carry

    lax.fori_loop(0, 16, start_rows, 0)

    def reversed_rows(buffer, k0):
        hi, lo = split(jnp.concatenate([buffer[15 - k0], buffer[(16 - k0) % 16]], axis=0))
        return dot(j_ref[...], hi) + dot(j_ref[...], lo)

    lanes128 = lax.broadcasted_iota(jnp.int32, (128, 128), 1)
    at_first = lanes128 % 64 == 0
    conj_sign = jnp.where(lanes128 < 64, 1.0, -1.0)
    has_pack = jnp.logical_and(par == 0, block == 0)

    def keep_low(ci, carry):
        slow[ci] = sbuf[ci + ci // 2 * 12]
        return carry

    lax.fori_loop(0, 4, keep_low, 0)

    @pl.when(has_pack)
    def _():
        def body(ci, carry):
            k0 = ci + ci // 2 * 12
            mirrored = reversed_rows(sbuf, k0) * conj_sign
            slow[ci] = jnp.where(at_first, 0.5 * (sbuf[k0] + mirrored), sbuf[k0])
            return carry

        lax.fori_loop(0, 4, body, 0)

    wait_all(fr, r3, my_r, ls.at[2], 16, partner)
    ky128 = column_waves(block, par, 128)
    turn128 = jnp.where(lanes128 < 64, -ky128, ky128)

    def flux_pair(q):
        first = fr[:, 0, q].reshape(128, 128)
        second = half_turn(fr[:, 1, q].reshape(128, 128)) * turn128
        return [
            jnp.where(lanes128 < 64, first, half_turn(second)),
            jnp.where(lanes128 < 64, half_turn(first), second),
        ]

    column_pass(flux_pair)
    ky8 = column_waves(block, par, 8)

    def flux_rows(kt, carry):
        rows, out = sixteen_at(kt)
        for k0 in range(16):
            places = 128 * k0 + kt * 8 + lax.broadcasted_iota(jnp.int32, (8, 128), 0)
            kx = waves_of(places)
            square = kx * kx + ky8 * ky8
            scale = DT / (1.0 + (DT * STIFF) * square * square)
            diverge = half_turn(out[k0][0]) * jnp.where(left, 1.0, kx) + out[k0][1] * jnp.where(left, -kx, 1.0)
            fin[k0, rows, :] = sbuf[k0, rows, :] - scale * diverge
        return carry

    lax.fori_loop(0, 16, flux_rows, 0)

    @pl.when(has_pack)
    def _():
        def body(k0, carry):
            mirrored = reversed_rows(fin, k0) * conj_sign
            zb[k0, 0:128, :] = jnp.where(at_first, 0.5 * (fin[k0] + mirrored), fin[k0])
            zb[k0, 128:256, :] = half_turn(fin[k0] - mirrored) * (0.5 * conj_sign)
            return carry

        lax.fori_loop(0, 16, body, 0)

        def back(k0, carry):
            fin[k0] = zb[k0, 0:128, :]
            return carry

        lax.fori_loop(0, 16, back, 0)

    home_b = (tm, block)
    home_m = (tm, 15 - block)
    same_home = block == space
    spans = ((2, 12), (0, 2), (14, 2))

    def out_copies(n):
        first, count = spans[n]
        src = fin.at[pl.ds(first, count)]
        dst = hr.at[par, pl.ds(first, count)]
        return (
            remote(src, dst, so.at[n], ro.at[par, n], home_b),
            remote(src, dst, so.at[3 + n], ro.at[par, n], home_m),
            pltpu.make_async_copy(src, dst, ls.at[3 + n]),
        )

    def begin_out(n):
        direct, mirror, local = out_copies(n)
        mirror.start()

        @pl.when(same_home)
        def _():
            local.start()

        @pl.when(jnp.logical_not(same_home))
        def _():
            direct.start()

    begin_out(0)
    def low_block(t):
        ci = t // 4
        return ci, ci + ci // 2 * 12, pl.multiple_of(t % 4 * 32, 32)

    def low_tables(t):
        ci, k0, first = low_block(t)
        places = 128 * k0 + first + lax.broadcasted_iota(jnp.int32, (32, 128), 0)
        kx = waves_of(places)
        ky = column_waves(block, par, 32)
        square = kx * kx + ky * ky
        gain = 1.0 / (1.0 + DT * (square * square * (1.0 / 3.0) - MEAN_MOBILITY * square))
        return gain, places != NG - 256

    def chain_out(t):
        return remote(dl.at[t], cr.at[my_slice], sc.at[t], rc.at[my_slice], chain_dev(t))

    def chain_back(t):
        return remote(co.at[t], cb.at[my_slice], sd.at[t], rd.at[my_slice], chain_dev(t))

    @pl.when(is_low)
    def _():
        def defects(t, carry):
            ci, k0, first = low_block(t)
            gain, keep = low_tables(t)
            gain = jnp.where(my_slice == 0, 0.0, gain)
            rows = pl.ds(first, 32)
            dl[t] = jnp.where(keep, fin[k0, rows, :] - gain * slow[ci, rows, :], 0.0)
            begin(t, my_slice, chain_out(t), dl.at[t], cr.at[my_slice], ls.at[6])
            return carry

        lax.fori_loop(0, 16, defects, 0)
        wait_all(cr, rc, my_slice, ls.at[6], 16, partner)
        gain, keep = low_tables(my_slice)

        def advance(t, current):
            current = gain * current + cr[t]
            co[t] = current
            begin(t, my_slice, chain_back(t), co.at[t], cb.at[my_slice], ls.at[7])
            return current

        lax.fori_loop(0, 16, advance, jnp.zeros((32, 128), F32))
        wait_all(cb, rd, my_slice, ls.at[7], 16, partner)

        def merge(t, carry):
            ci, k0, first = low_block(t)
            gain, keep = low_tables(t)
            rows = pl.ds(first, 32)
            fin[k0, rows, :] = jnp.where(keep, cb[t], fin[k0, rows, :])
            return carry

        lax.fori_loop(0, 16, merge, 0)

    begin_out(1)
    begin_out(2)
    extra_home = jnp.where(block == 0, 8, 16 - block)
    extra_copy = remote(ebuf, er, se.at[0], re_.at[0], (tm, extra_home))

    @pl.when(par == 0)
    def _():
        def body(k0, carry):
            tile = jnp.transpose(jnp.where(has_pack, zb[k0, 128:256, :], fin[k0]))
            ebuf[k0, 0:1, :] = tile[0:1, :]
            ebuf[k0, 1:2, :] = tile[64:65, :]
            return carry

        lax.fori_loop(0, 16, body, 0)
        extra_copy.start()


    is_mirror = space >= 8
    for source_par in range(2):
        local_here = jnp.logical_and(same_home, par == source_par)
        for n in range(3):
            first, count = spans[n]
            view = hr.at[source_par, pl.ds(first, count)]

            @pl.when(local_here)
            def _():
                pltpu.make_async_copy(view, view, ls.at[3 + n]).wait()

            @pl.when(jnp.logical_not(local_here))
            def _():
                remote(view, view, ro.at[source_par, n], ro.at[source_par, n], partner).wait_recv()

    @pl.when(is_mirror)
    def _():
        remote(er, er, re_.at[0], re_.at[0], partner).wait_recv()

        def body(k0, carry):
            rows = lax.broadcasted_iota(jnp.int32, (128, 128), 0)
            tile = jnp.where(rows == 0, er[k0, 0:1, :], jnp.where(rows == 64, er[k0, 1:2, :], 0.0))
            hr[0, k0] = jnp.where(at_first, jnp.transpose(tile), hr[0, k0])
            return carry

        lax.fori_loop(0, 16, body, 0)

    def ordered(k0, table):
        hi, lo = split(jnp.concatenate([hr[0, k0], hr[1, k0]], axis=1))
        return dot(hi, table) + dot(lo, table)

    def put(k0, values):
        rows = pl.ds(pl.multiple_of(k0 * 128, 128), 128)
        o_ref[0, 0, rows, :] = values[:, :128]
        o_ref[0, 1, rows, :] = values[:, 128:]

    @pl.when(jnp.logical_not(is_mirror))
    def _():
        def body(k0, carry):
            put(k0, ordered(k0, p_ref[0]))
            return carry

        lax.fori_loop(0, 16, body, 0)

    @pl.when(is_mirror)
    def _():
        def body(k0, carry):
            values = ordered(k0, p_ref[1])
            zb[k0, 0:128, :] = values[:, :128]
            zb[k0, 128:256, :] = values[:, 128:]
            return carry

        lax.fori_loop(0, 16, body, 0)

        def turn_rows(k0, carry):
            one, two = 15 - k0, (16 - k0) % 16
            upper = jnp.concatenate([zb[one, 0:128, :], zb[one, 128:256, :]], axis=1)
            lower = jnp.concatenate([zb[two, 0:128, :], zb[two, 128:256, :]], axis=1)
            hi, lo = split(jnp.concatenate([upper, lower], axis=0))
            put(k0, dot(j_ref[...], hi) + dot(j_ref[...], lo))
            return carry

        lax.fori_loop(0, 16, turn_rows, 0)

    def sent(k, carry):
        @pl.when(k != my_c)
        def _():
            t1_copy(k).wait_send()
            t3_copy(k).wait_send()

        @pl.when(k != my_r)
        def _():
            t2_copy(k).wait_send()

        return carry

    lax.fori_loop(0, 16, sent, 0)
    for n in range(3):
        direct, mirror, local = out_copies(n)
        mirror.wait_send()

        @pl.when(jnp.logical_not(same_home))
        def _():
            direct.wait_send()

    @pl.when(par == 0)
    def _():
        extra_copy.wait_send()

    @pl.when(is_low)
    def _():
        def body(t, carry):
            @pl.when(t != my_slice)
            def _():
                chain_out(t).wait_send()
                chain_back(t).wait_send()

            return carry

        lax.fori_loop(0, 16, body, 0)


def solution(mesh):
    tables = [
        forward_tables(),
        derivative_table(),
        column_tables(),
        lane_tables(),
        reversal_table(),
        order_table(),
    ]
    vmem = pl.BlockSpec(memory_space=pltpu.VMEM)
    anywhere = pl.BlockSpec(memory_space=pl.ANY)
    dma = pltpu.SemaphoreType.DMA

    def shards(starts, stress):
        return pl.pallas_call(
            kernel,
            out_shape=jax.ShapeDtypeStruct((1, 2, NG, 128), F32),
            in_specs=[vmem, vmem, anywhere, anywhere, anywhere, vmem, vmem, vmem],
            out_specs=vmem,
            scratch_shapes=[
                pltpu.VMEM((2, 2, HALF, HALF), BF16),
                pltpu.VMEM((768, NG), BF16),
                pltpu.VMEM((16, 512, 256), BF16),
                pltpu.VMEM((128, NG), F32),
                pltpu.VMEM((2, 128, NG), F32),
                pltpu.VMEM((2, 256, HALF), BF16),
                pltpu.VMEM((16, 16, 8, 128), F32),
                pltpu.VMEM((16, 16, 8, 128), F32),
                pltpu.VMEM((32, 128, 256), BF16),
                pltpu.VMEM((32, 128, 256), BF16),
                pltpu.VMEM((16, 384, 128), F32),
                pltpu.VMEM((16, 384, 128), F32),
                pltpu.VMEM((2, 1024, HALF), BF16),
                pltpu.VMEM((2, 512, HALF), BF16),
                pltpu.VMEM((16, 2, 16, 8, 128), F32),
                pltpu.VMEM((16, 2, 16, 8, 128), F32),
                pltpu.VMEM((16, 256, 128), F32),
                pltpu.VMEM((16, 128, 128), F32),
                pltpu.VMEM((4, 128, 128), F32),
                pltpu.VMEM((16, 128, 128), F32),
                pltpu.VMEM((16, 8, 128), F32),
                pltpu.VMEM((2, 16, 128, 128), F32),
                pltpu.VMEM((16, 8, 128), F32),
                pltpu.VMEM((16, 32, 128), F32),
                pltpu.VMEM((16, 32, 128), F32),
                pltpu.VMEM((16, 32, 128), F32),
                pltpu.VMEM((16, 32, 128), F32),
                dma((3,)),
                dma((16,)), dma((16,)), dma((16,)), dma((16,)), dma((16,)), dma((16,)),
                dma((6,)), dma((2, 3)), dma((1,)), dma((1,)),
                dma((16,)), dma((16,)), dma((16,)), dma((16,)), dma((8,)),
            ],
            compiler_params=pltpu.CompilerParams(
                collective_id=0, has_side_effects=True, vmem_limit_bytes=62 * 1024 * 1024
            ),
            name="parareal",
        )(starts, stress, *[jnp.asarray(table) for table in tables])

    return jax.shard_map(
        shards,
        mesh=mesh,
        in_specs=(P("tm", "space", None), P(None, "space", None)),
        out_specs=P("tm", None, None, "space"),
        check_vma=False,
    )
```

```python
import math

import jax
import jax.numpy as jnp
import ml_dtypes
import numpy as np
from jax import lax
from jax.experimental import pallas as pl
from jax.experimental.pallas import tpu as pltpu
from jax.sharding import PartitionSpec as P

NG = 2048
HALF = 1024
DT = 0.05
STIFF = 1.5
MEAN_MOBILITY = 0.25
MESH = pl.DeviceIdType.MESH
F32 = jnp.float32
BF16 = jnp.bfloat16


def split_np(values):
    hi = values.astype(np.float32).astype(ml_dtypes.bfloat16)
    lo = (values - hi.astype(np.float64)).astype(np.float32).astype(ml_dtypes.bfloat16)
    return hi, lo


def row_places():
    p = np.arange(128)
    return 16 * (p % 8) + p // 8


def forward_tables():
    y = np.arange(HALF)[:, None]
    tables = []
    for par in range(2):
        lane = np.arange(HALF)[None, :]
        block, slot, t = lane // 128, lane % 128 // 64, lane % 64
        ky = 128 * block + 2 * t + par
        angle = 2 * np.pi * ((ky * y) % NG) / NG
        table = np.where(slot == 0, np.cos(angle), -np.sin(angle))
        if par == 0:
            table[:, 64] = np.where(np.arange(HALF) % 2 == 0, 1.0, -1.0)
        tables.append(np.stack(split_np(table / math.sqrt(NG))))
    return np.stack(tables)


def derivative_table():
    k = np.arange(NG)
    wave = np.where(k < HALF, k, k - NG) * 2 * np.pi / NG
    wave[HALF] = 0.0
    local = row_places()
    target = local
    source = (128 * np.arange(16)[:, None] + local[None, :]).reshape(-1)
    gap = (target[:, None] - source[None, :]) % NG
    rows = [np.real(np.fft.ifft((1j * wave) ** m))[gap] for m in (1, 2, 3)]
    return np.concatenate(split_np(np.concatenate(rows)))


def column_tables():
    k1 = np.arange(128)[:, None]
    i = np.arange(128)[None, :]
    tables = []
    for q in range(16):
        angle = 2 * np.pi * ((q * k1 + 16 * i * k1) % NG) / NG
        c, s = np.cos(angle), np.sin(angle)
        table = np.block([[c, s], [-s, c]]) / math.sqrt(NG)
        tables.append(np.concatenate(split_np(table)))
    return np.stack(tables)


def lane_tables():
    tables = np.zeros((2, 256, 256))
    for par in range(2):
        for t in range(64):
            place = 2 * t + par
            mirrored = (128 - place) % 128
            for slot in range(2):
                source = par * 128 + slot * 64 + t
                tables[0, source, slot * 128 + place] = 1.0
                tables[1, source, slot * 128 + mirrored] = 1.0 - 2.0 * slot
    return tables.astype(ml_dtypes.bfloat16)


def reversal_table():
    table = np.zeros((128, 256))
    table[0, 128] = 1.0
    for k in range(1, 128):
        table[k, 128 - k] = 1.0
    return table.astype(ml_dtypes.bfloat16)


def order_table():
    table = np.zeros((128, 128))
    table[np.arange(128), row_places()] = 1.0
    return table.astype(ml_dtypes.bfloat16)


def split(values):
    hi = values.astype(BF16)
    return hi, (values - hi.astype(F32)).astype(BF16)


def dot(a, b):
    return jnp.dot(a, b, preferred_element_type=F32)


def dot_t(a, b):
    return lax.dot_general(a, b, (((1,), (1,)), ((), ())), preferred_element_type=F32)


def four(a, b, c, d):
    sr, si = a[0] + c[0], a[1] + c[1]
    dr, di = a[0] - c[0], a[1] - c[1]
    tr, ti = b[0] + d[0], b[1] + d[1]
    er, ei = b[0] - d[0], b[1] - d[1]
    return ((sr + tr, si + ti), (dr + ei, di - er), (sr - tr, si - ti), (dr - ei, di + er))


def turned(value, m):
    re, im = value
    if m == 0:
        return value
    if m == 4:
        return (im, -re)
    c, s = math.cos(2 * math.pi * m / 16), math.sin(2 * math.pi * m / 16)
    return (re * c + im * s, im * c - re * s)


def sixteen(values):
    stage = {}
    for q0 in range(4):
        parts = four(*[values[4 * q1 + q0] for q1 in range(4)])
        for ka in range(4):
            stage[ka, q0] = turned(parts[ka], q0 * ka)
    out = [None] * 16
    for ka in range(4):
        parts = four(*[stage[ka, q0] for q0 in range(4)])
        for kb in range(4):
            out[ka + 4 * kb] = parts[kb]
    return out


def waves_of(places):
    signed = jnp.where(places < HALF, places, places - NG)
    signed = jnp.where(places == HALF, 0, signed)
    return signed.astype(F32) * (2.0 * math.pi / NG)


def kernel(
    eta_ref, stress_ref, wf_hbm, d_hbm, l_hbm, p_ref, j_ref, q_ref, o_ref,
    wf, dm, lm, ep, sp, ub, sb1, xr, x2h, x2l, sb2, br,
    ib, fb, sb3, fr, zb, sbuf, slow, fin, ebuf, hr, er, dl, cr, co, cb,
    const_sem, s1, r1, s2, r2, s3, r3, so, ro, se, re_, sc, rc, sd, rd, ls,
):
    tm, space = lax.axis_index("tm"), lax.axis_index("space")
    x, zh, c = space // 4, space // 2 % 2, space % 2
    par = x // 2
    block = (x + par * (3 - 2 * x)) * 4 + zh * 2 + c
    my_r = space
    my_c = par * 8 + block
    my_slice = tm
    is_low = jnp.logical_and(zh == 0, block < 2)
    partner = (tm, (space + 1) % 16)

    def r_dev(s):
        return (tm, s)

    def c_dev(k):
        kp, kb = k // 8, k % 8
        xb = kb // 4
        return (tm, (xb + kp * (3 - 2 * xb)) * 4 + kb % 4)

    def chain_dev(t):
        return (t, space)

    def remote(src, dst, ss, rs, dev):
        return pltpu.make_async_remote_copy(
            src_ref=src, dst_ref=dst, send_sem=ss, recv_sem=rs, device_id=dev, device_id_type=MESH
        )

    barrier = pltpu.get_barrier_semaphore()

    def greet(n, carry):
        pl.semaphore_signal(barrier, inc=1, device_id=(tm, (space + n) % 16), device_id_type=MESH)
        pl.semaphore_signal(barrier, inc=1, device_id=((tm + n) % 16, space), device_id_type=MESH)
        return carry

    lax.fori_loop(1, 16, greet, 0)

    wf_copy = pltpu.make_async_copy(wf_hbm, wf, const_sem.at[0])
    d_copy = pltpu.make_async_copy(d_hbm, dm, const_sem.at[1])
    l_copy = pltpu.make_async_copy(l_hbm, lm, const_sem.at[2])
    wf_copy.start()

    lane = lax.broadcasted_iota(jnp.int32, (8, 128), 1)
    left = lane < 64
    t_lane = lane % 64
    sign = jnp.where(left, -1.0, 1.0)

    def half_turn(values):
        return pltpu.roll(values, 64, 1)

    def reorder(source, target):
        def body(n, carry):
            cols = pl.ds(pl.multiple_of(n * 256, 256), 256)
            values = source(cols)
            hi = values.astype(BF16)
            rest = values - hi.astype(F32)
            mid = rest.astype(BF16)
            last = (rest - mid.astype(F32)).astype(BF16)
            target[:, cols] = dot(q_ref[...], hi) + dot(q_ref[...], mid) + dot(q_ref[...], last)
            return carry

        lax.fori_loop(0, 8, body, 0)

    reorder(lambda cols: eta_ref[0, :, cols], ep)

    def fold_start(n, carry):
        rows = pl.ds(pl.multiple_of(n * 16, 16), 16)
        lo_rows = pl.ds(pl.multiple_of(n * 16 + 128, 16), 16)
        first, second = ep[rows, :HALF], ep[rows, HALF:]
        for parity, values in ((0, first + second), (1, first - second)):
            hi, lo = split(values)
            ub[parity, rows, :] = hi
            ub[parity, lo_rows, :] = lo
        return carry

    lax.fori_loop(0, 8, fold_start, 0)
    wf_copy.wait()
    d_copy.start()
    l_copy.start()
    pl.semaphore_wait(barrier, 30)

    def begin(k, me, make, src, dst, sem):
        @pl.when(k != me)
        def _():
            make.start()

        @pl.when(k == me)
        def _():
            pltpu.make_async_copy(src, dst, sem).start()

    def t1_copy(k):
        return remote(sb1.at[k], xr.at[my_r], s1.at[k], r1.at[my_r], c_dev(k))

    def forward_start(n, carry):
        parity = n // 4
        cols = pl.ds(pl.multiple_of(n % 4 * 256, 256), 256)
        both = dot(ub[parity], wf[parity, 0, :, cols])
        out = both[:128] + both[128:] + dot(ub[parity, :128, :], wf[parity, 1, :, cols])
        for side in range(2):
            k = parity * 8 + n % 4 * 2 + side
            sb1[k] = out[:, side * 128 : side * 128 + 128].reshape(16, 8, 128)
            begin(k, my_c, t1_copy(k), sb1.at[k], xr.at[my_r], ls.at[0])
        return carry

    lax.fori_loop(0, 8, forward_start, 0)

    def wait_all(buffer, sems, me, sem, count, dev):
        def body(s, carry):
            @pl.when(s != me)
            def _():
                remote(buffer.at[s], buffer.at[s], sems.at[s], sems.at[s], dev).wait_recv()

            @pl.when(s == me)
            def _():
                pltpu.make_async_copy(buffer.at[s], buffer.at[s], sem).wait()

            return carry

        lax.fori_loop(0, count, body, 0)

    wait_all(xr, r1, my_r, ls.at[0], 16, partner)

    def spread(n, carry):
        own = xr[n % 16].reshape(128, 128)
        following = xr[(n + 1) % 16].reshape(128, 128)
        hi, lo = split(jnp.concatenate([own, following], axis=1))
        x2h[n] = hi
        x2l[n] = lo
        return carry

    lax.fori_loop(0, 32, spread, 0)
    d_copy.wait()

    def t2_copy(s):
        return remote(sb2.at[s], br.at[my_c], s2.at[s], r2.at[my_c], r_dev(s))

    def derive(n, carry):
        s = (my_r // 2 + n) % 8 * 2
        xh = x2h[pl.ds(s, 16)].reshape(NG, 256)
        xl = x2l[pl.ds(s, 16)].reshape(NG, 256)
        both = dot(dm[...], xh)
        out = both[:384] + both[384:] + dot(dm[:384, :], xl)
        for side in range(2):
            sb2[s + side] = out[:, side * 128 : side * 128 + 128]
        begin(s, my_r, t2_copy(s), sb2.at[s], br.at[my_c], ls.at[1])
        return carry

    lax.fori_loop(0, 8, derive, 0)

    for f in range(2):
        reorder(lambda cols: stress_ref[f, :, cols], sp.at[f])

    l_copy.wait()

    def column_pass(pair):
        def body(q, carry):
            hi, lo = split(jnp.concatenate(pair(q), axis=0))
            both = dot(lm[q], hi)
            zb[q] = both[:256] + both[256:] + dot(lm[q, :256, :], lo)
            return carry

        lax.fori_loop(0, 16, body, 0)

    def sixteen_at(kt):
        rows = pl.ds(pl.multiple_of(kt * 8, 8), 8)
        im_rows = pl.ds(pl.multiple_of(128 + kt * 8, 8), 8)
        return rows, sixteen([(zb[q, rows, :], zb[q, im_rows, :]) for q in range(16)])

    def start_pair(q):
        values = xr[:, q].reshape(128, 128)
        return [values, half_turn(values)]

    column_pass(start_pair)

    def start_rows(kt, carry):
        rows, out = sixteen_at(kt)
        for k0 in range(16):
            sbuf[k0, rows, :] = jnp.where(left, out[k0][0], half_turn(out[k0][1]))
        return carry

    lax.fori_loop(0, 16, start_rows, 0)

    def reversed_rows(buffer, k0):
        hi, lo = split(jnp.concatenate([buffer[15 - k0], buffer[(16 - k0) % 16]], axis=0))
        return dot(j_ref[...], hi) + dot(j_ref[...], lo)

    lanes128 = lax.broadcasted_iota(jnp.int32, (128, 128), 1)
    at_first = lanes128 % 64 == 0
    conj_sign = jnp.where(lanes128 < 64, 1.0, -1.0)
    has_pack = jnp.logical_and(par == 0, block == 0)

    def keep_low(ci, carry):
        slow[ci] = sbuf[ci + ci // 2 * 12]
        return carry

    lax.fori_loop(0, 4, keep_low, 0)

    @pl.when(has_pack)
    def _():
        def body(ci, carry):
            k0 = ci + ci // 2 * 12
            mirrored = reversed_rows(sbuf, k0) * conj_sign
            slow[ci] = jnp.where(at_first, 0.5 * (sbuf[k0] + mirrored), sbuf[k0])
            return carry

        lax.fori_loop(0, 4, body, 0)

    def leave(make, me):
        def body(n, carry):
            @pl.when(2 * n != me)
            def _():
                make(2 * n).wait_send()

            return carry

        lax.fori_loop(0, 8, body, 0)

    def follow(make, me, ends, sem):
        def body(n, carry):
            k = (me // 2 + n) % 8 * 2 + 1
            src, dst = ends(k)
            begin(k, me, make(k), src, dst, sem)
            return carry

        lax.fori_loop(0, 8, body, 0)

    follow(t2_copy, my_r, lambda s: (sb2.at[s], br.at[my_c]), ls.at[1])
    wait_all(br, r2, my_c, ls.at[1], 16, partner)

    def column_waves(kb, kp, rows):
        lanes = lax.broadcasted_iota(jnp.int32, (rows, 128), 1) % 64
        return (128 * kb + 2 * lanes + kp).astype(F32) * (2.0 * math.pi / NG)

    def pack(k, carry):
        kp, kb = k // 8, k % 8
        ky = column_waves(kb, kp, 128)
        lanes = lax.broadcasted_iota(jnp.int32, (128, 128), 1)
        turn = jnp.where(lanes < 64, -ky, ky)
        weight = jnp.where(jnp.logical_and(k == 0, lanes % 64 == 0), 1.0, 2.0)
        x1, x2, x3 = br[k, 0:128, :], br[k, 128:256, :], br[k, 256:384, :]
        own = sb1[k].reshape(128, 128)
        cols = pl.ds(pl.multiple_of(kb * 128, 128), 128)
        fields = (
            x1,
            x3 - ky * ky * x1,
            half_turn(x2 - ky * ky * own) * turn,
            half_turn(own) * turn,
        )
        for f, values in enumerate(fields):
            hi, lo = split(values * weight)
            ib[kp, f * 128 : f * 128 + 128, cols] = hi
            ib[kp, 512 + f * 128 : 640 + f * 128, cols] = lo
        return carry

    lax.fori_loop(0, 16, pack, 0)

    def fluxes(n, carry):
        rows = pl.ds(pl.multiple_of(n * 256, 256), 256)
        sums = []
        for parity in range(2):
            both = dot_t(ib[parity], wf[parity, 0, rows, :])
            sums.append(both[:512] + both[512:] + dot_t(ib[parity, :512, :], wf[parity, 1, rows, :]))
        results = []
        for half in range(2):
            fields = sums[0] + sums[1] if half == 0 else sums[0] - sums[1]
            cols = pl.ds(pl.multiple_of(n * 256 + half * HALF, 256), 256)
            height = 1.0 + ep[:, cols]
            square = height * height
            mobility = square * height * (1.0 / 3.0)
            marangoni = square / ((1.0 + height) * (1.0 + height))
            shear = 0.5 * square
            results.append((
                mobility * fields[128:256] + marangoni * fields[0:128] + shear * sp[0, :, cols],
                mobility * fields[256:384] + marangoni * fields[384:512] + shear * sp[1, :, cols],
            ))
        for f in range(2):
            for parity in range(2):
                values = results[0][f] + results[1][f] if parity == 0 else results[0][f] - results[1][f]
                hi, lo = split(values)
                fb[parity, f * 128 : f * 128 + 128, rows] = hi
                fb[parity, 256 + f * 128 : 384 + f * 128, rows] = lo
        return carry

    lax.fori_loop(0, 4, fluxes, 0)

    def t3_copy(k):
        return remote(sb3.at[k], fr.at[my_r], s3.at[k], r3.at[my_r], c_dev(k))

    def forward_flux(n, carry):
        parity = n % 2
        cols = pl.ds(pl.multiple_of(n // 2 * 256, 256), 256)
        both = dot(fb[parity], wf[parity, 0, :, cols])
        out = both[:256] + both[256:] + dot(fb[parity, :256, :], wf[parity, 1, :, cols])
        for side in range(2):
            k = parity * 8 + n // 2 * 2 + side
            sb3[k] = out[:, side * 128 : side * 128 + 128].reshape(2, 16, 8, 128)
        k = parity * 8 + n // 2 * 2
        begin(k, my_c, t3_copy(k), sb3.at[k], fr.at[my_r], ls.at[2])
        return carry

    lax.fori_loop(0, 8, forward_flux, 0)

    leave(t3_copy, my_c)
    follow(t3_copy, my_c, lambda k: (sb3.at[k], fr.at[my_r]), ls.at[2])
    wait_all(fr, r3, my_r, ls.at[2], 16, partner)
    ky128 = column_waves(block, par, 128)
    turn128 = jnp.where(lanes128 < 64, -ky128, ky128)

    def flux_pair(q):
        first = fr[:, 0, q].reshape(128, 128)
        second = half_turn(fr[:, 1, q].reshape(128, 128)) * turn128
        return [
            jnp.where(lanes128 < 64, first, half_turn(second)),
            jnp.where(lanes128 < 64, half_turn(first), second),
        ]

    column_pass(flux_pair)
    ky8 = column_waves(block, par, 8)

    def flux_rows(kt, carry):
        rows, out = sixteen_at(kt)
        for k0 in range(16):
            places = 128 * k0 + kt * 8 + lax.broadcasted_iota(jnp.int32, (8, 128), 0)
            kx = waves_of(places)
            square = kx * kx + ky8 * ky8
            scale = DT / (1.0 + (DT * STIFF) * square * square)
            diverge = half_turn(out[k0][0]) * jnp.where(left, 1.0, kx) + out[k0][1] * jnp.where(left, -kx, 1.0)
            fin[k0, rows, :] = sbuf[k0, rows, :] - scale * diverge
        return carry

    lax.fori_loop(0, 16, flux_rows, 0)

    @pl.when(has_pack)
    def _():
        def body(k0, carry):
            mirrored = reversed_rows(fin, k0) * conj_sign
            zb[k0, 0:128, :] = jnp.where(at_first, 0.5 * (fin[k0] + mirrored), fin[k0])
            zb[k0, 128:256, :] = half_turn(fin[k0] - mirrored) * (0.5 * conj_sign)
            return carry

        lax.fori_loop(0, 16, body, 0)

        def back(k0, carry):
            fin[k0] = zb[k0, 0:128, :]
            return carry

        lax.fori_loop(0, 16, back, 0)

    home_b = (tm, block)
    home_m = (tm, 15 - block)
    same_home = block == space
    spans = ((2, 12), (0, 2), (14, 2))

    def out_copies(n):
        first, count = spans[n]
        src = fin.at[pl.ds(first, count)]
        dst = hr.at[par, pl.ds(first, count)]
        return (
            remote(src, dst, so.at[n], ro.at[par, n], home_b),
            remote(src, dst, so.at[3 + n], ro.at[par, n], home_m),
            pltpu.make_async_copy(src, dst, ls.at[3 + n]),
        )

    def begin_out(n):
        direct, mirror, local = out_copies(n)
        mirror.start()

        @pl.when(same_home)
        def _():
            local.start()

        @pl.when(jnp.logical_not(same_home))
        def _():
            direct.start()

    begin_out(0)
    def low_block(t):
        ci = t // 4
        return ci, ci + ci // 2 * 12, pl.multiple_of(t % 4 * 32, 32)

    def low_tables(t):
        ci, k0, first = low_block(t)
        places = 128 * k0 + first + lax.broadcasted_iota(jnp.int32, (32, 128), 0)
        kx = waves_of(places)
        ky = column_waves(block, par, 32)
        square = kx * kx + ky * ky
        gain = 1.0 / (1.0 + DT * (square * square * (1.0 / 3.0) - MEAN_MOBILITY * square))
        return gain, places != NG - 256

    def chain_out(t):
        return remote(dl.at[t], cr.at[my_slice], sc.at[t], rc.at[my_slice], chain_dev(t))

    def chain_back(t):
        return remote(co.at[t], cb.at[my_slice], sd.at[t], rd.at[my_slice], chain_dev(t))

    @pl.when(is_low)
    def _():
        def defects(t, carry):
            ci, k0, first = low_block(t)
            gain, keep = low_tables(t)
            gain = jnp.where(my_slice == 0, 0.0, gain)
            rows = pl.ds(first, 32)
            dl[t] = jnp.where(keep, fin[k0, rows, :] - gain * slow[ci, rows, :], 0.0)
            begin(t, my_slice, chain_out(t), dl.at[t], cr.at[my_slice], ls.at[6])
            return carry

        lax.fori_loop(0, 16, defects, 0)
        wait_all(cr, rc, my_slice, ls.at[6], 16, partner)
        gain, keep = low_tables(my_slice)

        def advance(t, current):
            current = gain * current + cr[t]
            co[t] = current
            begin(t, my_slice, chain_back(t), co.at[t], cb.at[my_slice], ls.at[7])
            return current

        lax.fori_loop(0, 16, advance, jnp.zeros((32, 128), F32))
        wait_all(cb, rd, my_slice, ls.at[7], 16, partner)

        def merge(t, carry):
            ci, k0, first = low_block(t)
            gain, keep = low_tables(t)
            rows = pl.ds(first, 32)
            fin[k0, rows, :] = jnp.where(keep, cb[t], fin[k0, rows, :])
            return carry

        lax.fori_loop(0, 16, merge, 0)

    begin_out(1)
    begin_out(2)
    extra_home = jnp.where(block == 0, 8, 16 - block)
    extra_copy = remote(ebuf, er, se.at[0], re_.at[0], (tm, extra_home))

    @pl.when(par == 0)
    def _():
        def body(k0, carry):
            tile = jnp.transpose(jnp.where(has_pack, zb[k0, 128:256, :], fin[k0]))
            ebuf[k0, 0:1, :] = tile[0:1, :]
            ebuf[k0, 1:2, :] = tile[64:65, :]
            return carry

        lax.fori_loop(0, 16, body, 0)
        extra_copy.start()


    is_mirror = space >= 8
    for source_par in range(2):
        local_here = jnp.logical_and(same_home, par == source_par)
        for n in range(3):
            first, count = spans[n]
            view = hr.at[source_par, pl.ds(first, count)]

            @pl.when(local_here)
            def _():
                pltpu.make_async_copy(view, view, ls.at[3 + n]).wait()

            @pl.when(jnp.logical_not(local_here))
            def _():
                remote(view, view, ro.at[source_par, n], ro.at[source_par, n], partner).wait_recv()

    @pl.when(is_mirror)
    def _():
        remote(er, er, re_.at[0], re_.at[0], partner).wait_recv()

        def body(k0, carry):
            rows = lax.broadcasted_iota(jnp.int32, (128, 128), 0)
            tile = jnp.where(rows == 0, er[k0, 0:1, :], jnp.where(rows == 64, er[k0, 1:2, :], 0.0))
            hr[0, k0] = jnp.where(at_first, jnp.transpose(tile), hr[0, k0])
            return carry

        lax.fori_loop(0, 16, body, 0)

    def ordered(k0, table):
        hi, lo = split(jnp.concatenate([hr[0, k0], hr[1, k0]], axis=1))
        return dot(hi, table) + dot(lo, table)

    def put(k0, values):
        rows = pl.ds(pl.multiple_of(k0 * 128, 128), 128)
        o_ref[0, 0, rows, :] = values[:, :128]
        o_ref[0, 1, rows, :] = values[:, 128:]

    @pl.when(jnp.logical_not(is_mirror))
    def _():
        def body(k0, carry):
            put(k0, ordered(k0, p_ref[0]))
            return carry

        lax.fori_loop(0, 16, body, 0)

    @pl.when(is_mirror)
    def _():
        def body(k0, carry):
            values = ordered(k0, p_ref[1])
            zb[k0, 0:128, :] = values[:, :128]
            zb[k0, 128:256, :] = values[:, 128:]
            return carry

        lax.fori_loop(0, 16, body, 0)

        def turn_rows(k0, carry):
            one, two = 15 - k0, (16 - k0) % 16
            upper = jnp.concatenate([zb[one, 0:128, :], zb[one, 128:256, :]], axis=1)
            lower = jnp.concatenate([zb[two, 0:128, :], zb[two, 128:256, :]], axis=1)
            hi, lo = split(jnp.concatenate([upper, lower], axis=0))
            put(k0, dot(j_ref[...], hi) + dot(j_ref[...], lo))
            return carry

        lax.fori_loop(0, 16, turn_rows, 0)

    def sent(k, carry):
        @pl.when(k != my_c)
        def _():
            t1_copy(k).wait_send()

        @pl.when(jnp.logical_and(k % 2 == 1, k != my_c))
        def _():
            t3_copy(k).wait_send()

        @pl.when(k != my_r)
        def _():
            t2_copy(k).wait_send()

        return carry

    lax.fori_loop(0, 16, sent, 0)
    for n in range(3):
        direct, mirror, local = out_copies(n)
        mirror.wait_send()

        @pl.when(jnp.logical_not(same_home))
        def _():
            direct.wait_send()

    @pl.when(par == 0)
    def _():
        extra_copy.wait_send()

    @pl.when(is_low)
    def _():
        def body(t, carry):
            @pl.when(t != my_slice)
            def _():
                chain_out(t).wait_send()
                chain_back(t).wait_send()

            return carry

        lax.fori_loop(0, 16, body, 0)


def solution(mesh):
    tables = [
        forward_tables(),
        derivative_table(),
        column_tables(),
        lane_tables(),
        reversal_table(),
        order_table(),
    ]
    vmem = pl.BlockSpec(memory_space=pltpu.VMEM)
    anywhere = pl.BlockSpec(memory_space=pl.ANY)
    dma = pltpu.SemaphoreType.DMA

    def shards(starts, stress):
        return pl.pallas_call(
            kernel,
            out_shape=jax.ShapeDtypeStruct((1, 2, NG, 128), F32),
            in_specs=[vmem, vmem, anywhere, anywhere, anywhere, vmem, vmem, vmem],
            out_specs=vmem,
            scratch_shapes=[
                pltpu.VMEM((2, 2, HALF, HALF), BF16),
                pltpu.VMEM((768, NG), BF16),
                pltpu.VMEM((16, 512, 256), BF16),
                pltpu.VMEM((128, NG), F32),
                pltpu.VMEM((2, 128, NG), F32),
                pltpu.VMEM((2, 256, HALF), BF16),
                pltpu.VMEM((16, 16, 8, 128), F32),
                pltpu.VMEM((16, 16, 8, 128), F32),
                pltpu.VMEM((32, 128, 256), BF16),
                pltpu.VMEM((32, 128, 256), BF16),
                pltpu.VMEM((16, 384, 128), F32),
                pltpu.VMEM((16, 384, 128), F32),
                pltpu.VMEM((2, 1024, HALF), BF16),
                pltpu.VMEM((2, 512, HALF), BF16),
                pltpu.VMEM((16, 2, 16, 8, 128), F32),
                pltpu.VMEM((16, 2, 16, 8, 128), F32),
                pltpu.VMEM((16, 256, 128), F32),
                pltpu.VMEM((16, 128, 128), F32),
                pltpu.VMEM((4, 128, 128), F32),
                pltpu.VMEM((16, 128, 128), F32),
                pltpu.VMEM((16, 8, 128), F32),
                pltpu.VMEM((2, 16, 128, 128), F32),
                pltpu.VMEM((16, 8, 128), F32),
                pltpu.VMEM((16, 32, 128), F32),
                pltpu.VMEM((16, 32, 128), F32),
                pltpu.VMEM((16, 32, 128), F32),
                pltpu.VMEM((16, 32, 128), F32),
                dma((3,)),
                dma((16,)), dma((16,)), dma((16,)), dma((16,)), dma((16,)), dma((16,)),
                dma((6,)), dma((2, 3)), dma((1,)), dma((1,)),
                dma((16,)), dma((16,)), dma((16,)), dma((16,)), dma((8,)),
            ],
            compiler_params=pltpu.CompilerParams(
                collective_id=0, has_side_effects=True, vmem_limit_bytes=62 * 1024 * 1024
            ),
            name="parareal",
        )(starts, stress, *[jnp.asarray(table) for table in tables])

    return jax.shard_map(
        shards,
        mesh=mesh,
        in_specs=(P("tm", "space", None), P(None, "space", None)),
        out_specs=P("tm", None, None, "space"),
        check_vma=False,
    )
```

```python
import math

import jax
import jax.numpy as jnp
import ml_dtypes
import numpy as np
from jax import lax
from jax.experimental import pallas as pl
from jax.experimental.pallas import tpu as pltpu
from jax.sharding import PartitionSpec as P

NG = 2048
HALF = 1024
DT = 0.05
STIFF = 1.5
MEAN_MOBILITY = 0.25
MESH = pl.DeviceIdType.MESH
F32 = jnp.float32
BF16 = jnp.bfloat16


def split_np(values):
    hi = values.astype(np.float32).astype(ml_dtypes.bfloat16)
    lo = (values - hi.astype(np.float64)).astype(np.float32).astype(ml_dtypes.bfloat16)
    return hi, lo


def row_places():
    p = np.arange(128)
    return 16 * (p % 8) + p // 8


def forward_tables():
    y = np.arange(HALF)[:, None]
    tables = []
    for par in range(2):
        lane = np.arange(HALF)[None, :]
        block, slot, t = lane // 128, lane % 128 // 64, lane % 64
        ky = 128 * block + 2 * t + par
        angle = 2 * np.pi * ((ky * y) % NG) / NG
        table = np.where(slot == 0, np.cos(angle), -np.sin(angle))
        if par == 0:
            table[:, 64] = np.where(np.arange(HALF) % 2 == 0, 1.0, -1.0)
        tables.append(np.stack(split_np(table / math.sqrt(NG))))
    return np.stack(tables)


def derivative_table():
    k = np.arange(NG)
    wave = np.where(k < HALF, k, k - NG) * 2 * np.pi / NG
    wave[HALF] = 0.0
    local = row_places()
    target = local
    source = (128 * np.arange(16)[:, None] + local[None, :]).reshape(-1)
    gap = (target[:, None] - source[None, :]) % NG
    rows = [np.real(np.fft.ifft((1j * wave) ** m))[gap] for m in (1, 2, 3)]
    return np.concatenate(split_np(np.concatenate(rows)))


def column_tables():
    k1 = np.arange(128)[:, None]
    i = np.arange(128)[None, :]
    tables = []
    for q in range(16):
        angle = 2 * np.pi * ((q * k1 + 16 * i * k1) % NG) / NG
        c, s = np.cos(angle), np.sin(angle)
        table = np.block([[c, s], [-s, c]]) / math.sqrt(NG)
        tables.append(np.concatenate(split_np(table)))
    return np.stack(tables)


def lane_tables():
    tables = np.zeros((2, 256, 256))
    for par in range(2):
        for t in range(64):
            place = 2 * t + par
            mirrored = (128 - place) % 128
            for slot in range(2):
                source = par * 128 + slot * 64 + t
                tables[0, source, slot * 128 + place] = 1.0
                tables[1, source, slot * 128 + mirrored] = 1.0 - 2.0 * slot
    return tables.astype(ml_dtypes.bfloat16)


def reversal_table():
    table = np.zeros((128, 256))
    table[0, 128] = 1.0
    for k in range(1, 128):
        table[k, 128 - k] = 1.0
    return table.astype(ml_dtypes.bfloat16)


def order_table():
    table = np.zeros((128, 128))
    table[np.arange(128), row_places()] = 1.0
    return table.astype(ml_dtypes.bfloat16)


def split(values):
    hi = values.astype(BF16)
    return hi, (values - hi.astype(F32)).astype(BF16)


def dot(a, b):
    return jnp.dot(a, b, preferred_element_type=F32)


def dot_t(a, b):
    return lax.dot_general(a, b, (((1,), (1,)), ((), ())), preferred_element_type=F32)


def four(a, b, c, d):
    sr, si = a[0] + c[0], a[1] + c[1]
    dr, di = a[0] - c[0], a[1] - c[1]
    tr, ti = b[0] + d[0], b[1] + d[1]
    er, ei = b[0] - d[0], b[1] - d[1]
    return ((sr + tr, si + ti), (dr + ei, di - er), (sr - tr, si - ti), (dr - ei, di + er))


def turned(value, m):
    re, im = value
    if m == 0:
        return value
    if m == 4:
        return (im, -re)
    c, s = math.cos(2 * math.pi * m / 16), math.sin(2 * math.pi * m / 16)
    return (re * c + im * s, im * c - re * s)


def sixteen(values):
    stage = {}
    for q0 in range(4):
        parts = four(*[values[4 * q1 + q0] for q1 in range(4)])
        for ka in range(4):
            stage[ka, q0] = turned(parts[ka], q0 * ka)
    out = [None] * 16
    for ka in range(4):
        parts = four(*[stage[ka, q0] for q0 in range(4)])
        for kb in range(4):
            out[ka + 4 * kb] = parts[kb]
    return out


def waves_of(places):
    signed = jnp.where(places < HALF, places, places - NG)
    signed = jnp.where(places == HALF, 0, signed)
    return signed.astype(F32) * (2.0 * math.pi / NG)


def kernel(
    eta_ref, stress_ref, wf_hbm, d_hbm, l_hbm, p_ref, j_ref, q_ref, o_ref,
    wf, dm, lm, ep, sp, ub, sb1, xr, x2h, x2l, sb2, br,
    ib, fb, sb3, fr, zb, sbuf, slow, fin, ebuf, hr, er, dl, cr, co, cb,
    const_sem, s1, r1, s2, r2, s3, r3, so, ro, se, re_, sc, rc, sd, rd, ls,
):
    tm, space = lax.axis_index("tm"), lax.axis_index("space")
    x, zh, c = space // 4, space // 2 % 2, space % 2
    par = x // 2
    block = (x + par * (3 - 2 * x)) * 4 + zh * 2 + c
    my_r = space
    my_c = par * 8 + block
    my_slice = tm
    is_low = jnp.logical_and(zh == 0, block < 2)
    partner = (tm, (space + 1) % 16)

    def r_dev(s):
        return (tm, s)

    def c_dev(k):
        kp, kb = k // 8, k % 8
        xb = kb // 4
        return (tm, (xb + kp * (3 - 2 * xb)) * 4 + kb % 4)

    def chain_dev(t):
        return (t, space)

    def remote(src, dst, ss, rs, dev):
        return pltpu.make_async_remote_copy(
            src_ref=src, dst_ref=dst, send_sem=ss, recv_sem=rs, device_id=dev, device_id_type=MESH
        )

    barrier = pltpu.get_barrier_semaphore()

    def greet(n, carry):
        pl.semaphore_signal(barrier, inc=1, device_id=(tm, (space + n) % 16), device_id_type=MESH)
        pl.semaphore_signal(barrier, inc=1, device_id=((tm + n) % 16, space), device_id_type=MESH)
        return carry

    lax.fori_loop(1, 16, greet, 0)

    wf_copy = pltpu.make_async_copy(wf_hbm, wf, const_sem.at[0])
    d_copy = pltpu.make_async_copy(d_hbm, dm, const_sem.at[1])
    l_copy = pltpu.make_async_copy(l_hbm, lm, const_sem.at[2])
    wf_copy.start()

    lane = lax.broadcasted_iota(jnp.int32, (8, 128), 1)
    left = lane < 64
    t_lane = lane % 64
    sign = jnp.where(left, -1.0, 1.0)

    def half_turn(values):
        return pltpu.roll(values, 64, 1)

    def reorder(source, target):
        def body(n, carry):
            cols = pl.ds(pl.multiple_of(n * 256, 256), 256)
            values = source(cols)
            hi = values.astype(BF16)
            rest = values - hi.astype(F32)
            mid = rest.astype(BF16)
            last = (rest - mid.astype(F32)).astype(BF16)
            target[:, cols] = dot(q_ref[...], hi) + dot(q_ref[...], mid) + dot(q_ref[...], last)
            return carry

        lax.fori_loop(0, 8, body, 0)

    reorder(lambda cols: eta_ref[0, :, cols], ep)

    def fold_start(n, carry):
        rows = pl.ds(pl.multiple_of(n * 16, 16), 16)
        lo_rows = pl.ds(pl.multiple_of(n * 16 + 128, 16), 16)
        first, second = ep[rows, :HALF], ep[rows, HALF:]
        for parity, values in ((0, first + second), (1, first - second)):
            hi, lo = split(values)
            ub[parity, rows, :] = hi
            ub[parity, lo_rows, :] = lo
        return carry

    lax.fori_loop(0, 8, fold_start, 0)
    wf_copy.wait()
    d_copy.start()
    l_copy.start()
    pl.semaphore_wait(barrier, 30)

    def begin(k, me, make, src, dst, sem):
        @pl.when(k != me)
        def _():
            make.start()

        @pl.when(k == me)
        def _():
            pltpu.make_async_copy(src, dst, sem).start()

    def t1_copy(k):
        return remote(sb1.at[k], xr.at[my_r], s1.at[k], r1.at[my_r], c_dev(k))

    def forward_start(n, carry):
        parity = n // 4
        cols = pl.ds(pl.multiple_of(n % 4 * 256, 256), 256)
        both = dot(ub[parity], wf[parity, 0, :, cols])
        out = both[:128] + both[128:] + dot(ub[parity, :128, :], wf[parity, 1, :, cols])
        for side in range(2):
            k = parity * 8 + n % 4 * 2 + side
            sb1[k] = out[:, side * 128 : side * 128 + 128].reshape(16, 8, 128)
            begin(k, my_c, t1_copy(k), sb1.at[k], xr.at[my_r], ls.at[0])
        return carry

    lax.fori_loop(0, 8, forward_start, 0)

    def wait_all(buffer, sems, me, sem, count, dev):
        def body(s, carry):
            @pl.when(s != me)
            def _():
                remote(buffer.at[s], buffer.at[s], sems.at[s], sems.at[s], dev).wait_recv()

            @pl.when(s == me)
            def _():
                pltpu.make_async_copy(buffer.at[s], buffer.at[s], sem).wait()

            return carry

        lax.fori_loop(0, count, body, 0)

    wait_all(xr, r1, my_r, ls.at[0], 16, partner)

    def spread(n, carry):
        own = xr[n % 16].reshape(128, 128)
        following = xr[(n + 1) % 16].reshape(128, 128)
        hi, lo = split(jnp.concatenate([own, following], axis=1))
        x2h[n] = hi
        x2l[n] = lo
        return carry

    lax.fori_loop(0, 32, spread, 0)
    d_copy.wait()

    def t2_copy(s):
        return remote(sb2.at[s], br.at[my_c], s2.at[s], r2.at[my_c], r_dev(s))

    def derive(n, carry):
        s = (my_r // 2 + n) % 8 * 2
        xh = x2h[pl.ds(s, 16)].reshape(NG, 256)
        xl = x2l[pl.ds(s, 16)].reshape(NG, 256)
        both = dot(dm[...], xh)
        out = both[:384] + both[384:] + dot(dm[:384, :], xl)
        for side in range(2):
            sb2[s + side] = out[:, side * 128 : side * 128 + 128]
        begin(s, my_r, t2_copy(s), sb2.at[s], br.at[my_c], ls.at[1])
        return carry

    lax.fori_loop(0, 8, derive, 0)

    for f in range(2):
        reorder(lambda cols: stress_ref[f, :, cols], sp.at[f])

    l_copy.wait()

    def column_pass(pair):
        def body(q, carry):
            hi, lo = split(jnp.concatenate(pair(q), axis=0))
            both = dot(lm[q], hi)
            zb[q] = both[:256] + both[256:] + dot(lm[q, :256, :], lo)
            return carry

        lax.fori_loop(0, 16, body, 0)

    def sixteen_at(kt):
        rows = pl.ds(pl.multiple_of(kt * 8, 8), 8)
        im_rows = pl.ds(pl.multiple_of(128 + kt * 8, 8), 8)
        return rows, sixteen([(zb[q, rows, :], zb[q, im_rows, :]) for q in range(16)])

    def start_pair(q):
        values = xr[:, q].reshape(128, 128)
        return [values, half_turn(values)]

    column_pass(start_pair)

    def start_rows(kt, carry):
        rows, out = sixteen_at(kt)
        for k0 in range(16):
            sbuf[k0, rows, :] = jnp.where(left, out[k0][0], half_turn(out[k0][1]))
        return carry

    lax.fori_loop(0, 16, start_rows, 0)

    def reversed_rows(buffer, k0):
        hi, lo = split(jnp.concatenate([buffer[15 - k0], buffer[(16 - k0) % 16]], axis=0))
        return dot(j_ref[...], hi) + dot(j_ref[...], lo)

    lanes128 = lax.broadcasted_iota(jnp.int32, (128, 128), 1)
    at_first = lanes128 % 64 == 0
    conj_sign = jnp.where(lanes128 < 64, 1.0, -1.0)
    has_pack = jnp.logical_and(par == 0, block == 0)

    def keep_low(ci, carry):
        slow[ci] = sbuf[ci + ci // 2 * 12]
        return carry

    lax.fori_loop(0, 4, keep_low, 0)

    @pl.when(has_pack)
    def _():
        def body(ci, carry):
            k0 = ci + ci // 2 * 12
            mirrored = reversed_rows(sbuf, k0) * conj_sign
            slow[ci] = jnp.where(at_first, 0.5 * (sbuf[k0] + mirrored), sbuf[k0])
            return carry

        lax.fori_loop(0, 4, body, 0)

    def leave(make, me):
        def body(n, carry):
            @pl.when(2 * n != me)
            def _():
                make(2 * n).wait_send()

            return carry

        lax.fori_loop(0, 8, body, 0)

    def follow(make, me, ends, sem):
        def body(n, carry):
            k = (me // 2 + n) % 8 * 2 + 1
            src, dst = ends(k)
            begin(k, me, make(k), src, dst, sem)
            return carry

        lax.fori_loop(0, 8, body, 0)

    follow(t2_copy, my_r, lambda s: (sb2.at[s], br.at[my_c]), ls.at[1])
    wait_all(br, r2, my_c, ls.at[1], 16, partner)

    def column_waves(kb, kp, rows):
        lanes = lax.broadcasted_iota(jnp.int32, (rows, 128), 1) % 64
        return (128 * kb + 2 * lanes + kp).astype(F32) * (2.0 * math.pi / NG)

    def pack(k, carry):
        kp, kb = k // 8, k % 8
        ky = column_waves(kb, kp, 128)
        lanes = lax.broadcasted_iota(jnp.int32, (128, 128), 1)
        turn = jnp.where(lanes < 64, -ky, ky)
        weight = jnp.where(jnp.logical_and(k == 0, lanes % 64 == 0), 1.0, 2.0)
        x1, x2, x3 = br[k, 0:128, :], br[k, 128:256, :], br[k, 256:384, :]
        own = sb1[k].reshape(128, 128)
        cols = pl.ds(pl.multiple_of(kb * 128, 128), 128)
        fields = (
            x1,
            x3 - ky * ky * x1,
            half_turn(x2 - ky * ky * own) * turn,
            half_turn(own) * turn,
        )
        for f, values in enumerate(fields):
            hi, lo = split(values * weight)
            ib[kp, f * 128 : f * 128 + 128, cols] = hi
            ib[kp, 512 + f * 128 : 640 + f * 128, cols] = lo
        return carry

    lax.fori_loop(0, 16, pack, 0)

    def fluxes(n, carry):
        rows = pl.ds(pl.multiple_of(n * 256, 256), 256)
        sums = []
        for parity in range(2):
            both = dot_t(ib[parity], wf[parity, 0, rows, :])
            sums.append(both[:512] + both[512:] + dot_t(ib[parity, :512, :], wf[parity, 1, rows, :]))
        results = []
        for half in range(2):
            fields = sums[0] + sums[1] if half == 0 else sums[0] - sums[1]
            cols = pl.ds(pl.multiple_of(n * 256 + half * HALF, 256), 256)
            height = 1.0 + ep[:, cols]
            square = height * height
            mobility = square * height * (1.0 / 3.0)
            marangoni = square / ((1.0 + height) * (1.0 + height))
            shear = 0.5 * square
            results.append((
                mobility * fields[128:256] + marangoni * fields[0:128] + shear * sp[0, :, cols],
                mobility * fields[256:384] + marangoni * fields[384:512] + shear * sp[1, :, cols],
            ))
        for f in range(2):
            for parity in range(2):
                values = results[0][f] + results[1][f] if parity == 0 else results[0][f] - results[1][f]
                hi, lo = split(values)
                fb[parity, f * 128 : f * 128 + 128, rows] = hi
                fb[parity, 256 + f * 128 : 384 + f * 128, rows] = lo
        return carry

    lax.fori_loop(0, 4, fluxes, 0)

    def t3_copy(k):
        return remote(sb3.at[k], fr.at[my_r], s3.at[k], r3.at[my_r], c_dev(k))

    def forward_flux(n, carry):
        parity = n % 2
        cols = pl.ds(pl.multiple_of(n // 2 * 256, 256), 256)
        both = dot(fb[parity], wf[parity, 0, :, cols])
        out = both[:256] + both[256:] + dot(fb[parity, :256, :], wf[parity, 1, :, cols])
        for side in range(2):
            k = parity * 8 + n // 2 * 2 + side
            sb3[k] = out[:, side * 128 : side * 128 + 128].reshape(2, 16, 8, 128)
        k = parity * 8 + n // 2 * 2
        begin(k, my_c, t3_copy(k), sb3.at[k], fr.at[my_r], ls.at[2])
        return carry

    lax.fori_loop(0, 8, forward_flux, 0)

    leave(t3_copy, my_c)
    follow(t3_copy, my_c, lambda k: (sb3.at[k], fr.at[my_r]), ls.at[2])
    wait_all(fr, r3, my_r, ls.at[2], 16, partner)
    ky128 = column_waves(block, par, 128)
    turn128 = jnp.where(lanes128 < 64, -ky128, ky128)

    def flux_pair(q):
        first = fr[:, 0, q].reshape(128, 128)
        second = half_turn(fr[:, 1, q].reshape(128, 128)) * turn128
        return [
            jnp.where(lanes128 < 64, first, half_turn(second)),
            jnp.where(lanes128 < 64, half_turn(first), second),
        ]

    column_pass(flux_pair)
    ky8 = column_waves(block, par, 8)

    def flux_rows(kt, carry):
        rows, out = sixteen_at(kt)
        for k0 in range(16):
            places = 128 * k0 + kt * 8 + lax.broadcasted_iota(jnp.int32, (8, 128), 0)
            kx = waves_of(places)
            square = kx * kx + ky8 * ky8
            scale = DT / (1.0 + (DT * STIFF) * square * square)
            diverge = half_turn(out[k0][0]) * jnp.where(left, 1.0, kx) + out[k0][1] * jnp.where(left, -kx, 1.0)
            fin[k0, rows, :] = sbuf[k0, rows, :] - scale * diverge
        return carry

    lax.fori_loop(0, 16, flux_rows, 0)

    @pl.when(has_pack)
    def _():
        def body(k0, carry):
            mirrored = reversed_rows(fin, k0) * conj_sign
            zb[k0, 0:128, :] = jnp.where(at_first, 0.5 * (fin[k0] + mirrored), fin[k0])
            zb[k0, 128:256, :] = half_turn(fin[k0] - mirrored) * (0.5 * conj_sign)
            return carry

        lax.fori_loop(0, 16, body, 0)

        def back(k0, carry):
            fin[k0] = zb[k0, 0:128, :]
            return carry

        lax.fori_loop(0, 16, back, 0)

    home_b = (tm, block)
    home_m = (tm, 15 - block)
    same_home = block == space
    spans = ((2, 12), (0, 2), (14, 2))

    def out_copies(n):
        first, count = spans[n]
        src = fin.at[pl.ds(first, count)]
        dst = hr.at[par, pl.ds(first, count)]
        return (
            remote(src, dst, so.at[n], ro.at[par, n], home_b),
            remote(src, dst, so.at[3 + n], ro.at[par, n], home_m),
            pltpu.make_async_copy(src, dst, ls.at[3 + n]),
        )

    def begin_out(n):
        direct, mirror, local = out_copies(n)
        mirror.start()

        @pl.when(same_home)
        def _():
            local.start()

        @pl.when(jnp.logical_not(same_home))
        def _():
            direct.start()

    begin_out(0)
    def low_block(t):
        ci = t // 4
        return ci, ci + ci // 2 * 12, pl.multiple_of(t % 4 * 32, 32)

    def low_tables(t):
        ci, k0, first = low_block(t)
        places = 128 * k0 + first + lax.broadcasted_iota(jnp.int32, (32, 128), 0)
        kx = waves_of(places)
        ky = column_waves(block, par, 32)
        square = kx * kx + ky * ky
        gain = 1.0 / (1.0 + DT * (square * square * (1.0 / 3.0) - MEAN_MOBILITY * square))
        return gain, places != NG - 256

    def chain_out(t):
        return remote(dl.at[t], cr.at[my_slice], sc.at[t], rc.at[my_slice], chain_dev(t))

    def chain_back(t):
        return remote(co.at[t], cb.at[my_slice], sd.at[t], rd.at[my_slice], chain_dev(t))

    @pl.when(is_low)
    def _():
        def defects(t, carry):
            ci, k0, first = low_block(t)
            gain, keep = low_tables(t)
            gain = jnp.where(my_slice == 0, 0.0, gain)
            rows = pl.ds(first, 32)
            dl[t] = jnp.where(keep, fin[k0, rows, :] - gain * slow[ci, rows, :], 0.0)
            begin(t, my_slice, chain_out(t), dl.at[t], cr.at[my_slice], ls.at[6])
            return carry

        lax.fori_loop(0, 16, defects, 0)
        wait_all(cr, rc, my_slice, ls.at[6], 16, partner)
        gain, keep = low_tables(my_slice)

        def advance(t, current):
            current = gain * current + cr[t]
            co[t] = current
            begin(t, my_slice, chain_back(t), co.at[t], cb.at[my_slice], ls.at[7])
            return current

        lax.fori_loop(0, 16, advance, jnp.zeros((32, 128), F32))
        wait_all(cb, rd, my_slice, ls.at[7], 16, partner)

        def merge(t, carry):
            ci, k0, first = low_block(t)
            gain, keep = low_tables(t)
            rows = pl.ds(first, 32)
            fin[k0, rows, :] = jnp.where(keep, cb[t], fin[k0, rows, :])
            return carry

        lax.fori_loop(0, 16, merge, 0)

    begin_out(1)
    begin_out(2)
    extra_home = jnp.where(block == 0, 8, 16 - block)
    extra_copy = remote(ebuf, er, se.at[0], re_.at[0], (tm, extra_home))

    @pl.when(par == 0)
    def _():
        def body(k0, carry):
            tile = jnp.transpose(jnp.where(has_pack, zb[k0, 128:256, :], fin[k0]))
            ebuf[k0, 0:1, :] = tile[0:1, :]
            ebuf[k0, 1:2, :] = tile[64:65, :]
            return carry

        lax.fori_loop(0, 16, body, 0)
        extra_copy.start()


    is_mirror = space >= 8

    def arrived(n):
        first, count = spans[n]
        for source_par in range(2):
            local_here = jnp.logical_and(same_home, par == source_par)
            view = hr.at[source_par, pl.ds(first, count)]

            @pl.when(local_here)
            def _():
                pltpu.make_async_copy(view, view, ls.at[3 + n]).wait()

            @pl.when(jnp.logical_not(local_here))
            def _():
                remote(view, view, ro.at[source_par, n], ro.at[source_par, n], partner).wait_recv()

    def ordered(k0, table):
        hi, lo = split(jnp.concatenate([hr[0, k0], hr[1, k0]], axis=1))
        return dot(hi, table) + dot(lo, table)

    def put(k0, values):
        rows = pl.ds(pl.multiple_of(k0 * 128, 128), 128)
        o_ref[0, 0, rows, :] = values[:, :128]
        o_ref[0, 1, rows, :] = values[:, 128:]

    def order_span(n):
        first, count = spans[n]

        @pl.when(jnp.logical_not(is_mirror))
        def _():
            def body(k0, carry):
                put(k0, ordered(k0, p_ref[0]))
                return carry

            lax.fori_loop(first, first + count, body, 0)

        @pl.when(is_mirror)
        def _():
            def body(k0, carry):
                values = ordered(k0, p_ref[1])
                zb[k0, 0:128, :] = values[:, :128]
                zb[k0, 128:256, :] = values[:, 128:]
                return carry

            lax.fori_loop(first, first + count, body, 0)

    for n in range(3):
        arrived(n)
        order_span(n)

    @pl.when(is_mirror)
    def _():
        remote(er, er, re_.at[0], re_.at[0], partner).wait_recv()

        def body(k0, carry):
            rows = lax.broadcasted_iota(jnp.int32, (128, 128), 0)
            tile = jnp.where(rows == 0, er[k0, 0:1, :], jnp.where(rows == 64, er[k0, 1:2, :], 0.0))
            extra = jnp.transpose(tile)
            zb[k0, 0:128, :] = jnp.where(lanes128 == 0, extra, zb[k0, 0:128, :])
            zb[k0, 128:256, :] = jnp.where(lanes128 == 0, -half_turn(extra), zb[k0, 128:256, :])
            return carry

        lax.fori_loop(0, 16, body, 0)

        def turn_rows(k0, carry):
            one, two = 15 - k0, (16 - k0) % 16
            upper = jnp.concatenate([zb[one, 0:128, :], zb[one, 128:256, :]], axis=1)
            lower = jnp.concatenate([zb[two, 0:128, :], zb[two, 128:256, :]], axis=1)
            hi, lo = split(jnp.concatenate([upper, lower], axis=0))
            put(k0, dot(j_ref[...], hi) + dot(j_ref[...], lo))
            return carry

        lax.fori_loop(0, 16, turn_rows, 0)

    def sent(k, carry):
        @pl.when(k != my_c)
        def _():
            t1_copy(k).wait_send()

        @pl.when(jnp.logical_and(k % 2 == 1, k != my_c))
        def _():
            t3_copy(k).wait_send()

        @pl.when(k != my_r)
        def _():
            t2_copy(k).wait_send()

        return carry

    lax.fori_loop(0, 16, sent, 0)
    for n in range(3):
        direct, mirror, local = out_copies(n)
        mirror.wait_send()

        @pl.when(jnp.logical_not(same_home))
        def _():
            direct.wait_send()

    @pl.when(par == 0)
    def _():
        extra_copy.wait_send()

    @pl.when(is_low)
    def _():
        def body(t, carry):
            @pl.when(t != my_slice)
            def _():
                chain_out(t).wait_send()
                chain_back(t).wait_send()

            return carry

        lax.fori_loop(0, 16, body, 0)


def solution(mesh):
    tables = [
        forward_tables(),
        derivative_table(),
        column_tables(),
        lane_tables(),
        reversal_table(),
        order_table(),
    ]
    vmem = pl.BlockSpec(memory_space=pltpu.VMEM)
    anywhere = pl.BlockSpec(memory_space=pl.ANY)
    dma = pltpu.SemaphoreType.DMA

    def shards(starts, stress):
        return pl.pallas_call(
            kernel,
            out_shape=jax.ShapeDtypeStruct((1, 2, NG, 128), F32),
            in_specs=[vmem, vmem, anywhere, anywhere, anywhere, vmem, vmem, vmem],
            out_specs=vmem,
            scratch_shapes=[
                pltpu.VMEM((2, 2, HALF, HALF), BF16),
                pltpu.VMEM((768, NG), BF16),
                pltpu.VMEM((16, 512, 256), BF16),
                pltpu.VMEM((128, NG), F32),
                pltpu.VMEM((2, 128, NG), F32),
                pltpu.VMEM((2, 256, HALF), BF16),
                pltpu.VMEM((16, 16, 8, 128), F32),
                pltpu.VMEM((16, 16, 8, 128), F32),
                pltpu.VMEM((32, 128, 256), BF16),
                pltpu.VMEM((32, 128, 256), BF16),
                pltpu.VMEM((16, 384, 128), F32),
                pltpu.VMEM((16, 384, 128), F32),
                pltpu.VMEM((2, 1024, HALF), BF16),
                pltpu.VMEM((2, 512, HALF), BF16),
                pltpu.VMEM((16, 2, 16, 8, 128), F32),
                pltpu.VMEM((16, 2, 16, 8, 128), F32),
                pltpu.VMEM((16, 256, 128), F32),
                pltpu.VMEM((16, 128, 128), F32),
                pltpu.VMEM((4, 128, 128), F32),
                pltpu.VMEM((16, 128, 128), F32),
                pltpu.VMEM((16, 8, 128), F32),
                pltpu.VMEM((2, 16, 128, 128), F32),
                pltpu.VMEM((16, 8, 128), F32),
                pltpu.VMEM((16, 32, 128), F32),
                pltpu.VMEM((16, 32, 128), F32),
                pltpu.VMEM((16, 32, 128), F32),
                pltpu.VMEM((16, 32, 128), F32),
                dma((3,)),
                dma((16,)), dma((16,)), dma((16,)), dma((16,)), dma((16,)), dma((16,)),
                dma((6,)), dma((2, 3)), dma((1,)), dma((1,)),
                dma((16,)), dma((16,)), dma((16,)), dma((16,)), dma((8,)),
            ],
            compiler_params=pltpu.CompilerParams(
                collective_id=0, has_side_effects=True, vmem_limit_bytes=62 * 1024 * 1024
            ),
            name="parareal",
        )(starts, stress, *[jnp.asarray(table) for table in tables])

    return jax.shard_map(
        shards,
        mesh=mesh,
        in_specs=(P("tm", "space", None), P(None, "space", None)),
        out_specs=P("tm", None, None, "space"),
        check_vma=False,
    )
```

```python
import math

import jax
import jax.numpy as jnp
import ml_dtypes
import numpy as np
from jax import lax
from jax.experimental import pallas as pl
from jax.experimental.pallas import tpu as pltpu
from jax.sharding import PartitionSpec as P

NG = 2048
HALF = 1024
DT = 0.05
STIFF = 1.5
MEAN_MOBILITY = 0.25
MESH = pl.DeviceIdType.MESH
F32 = jnp.float32
BF16 = jnp.bfloat16


def split_np(values):
    hi = values.astype(np.float32).astype(ml_dtypes.bfloat16)
    lo = (values - hi.astype(np.float64)).astype(np.float32).astype(ml_dtypes.bfloat16)
    return hi, lo


def row_places():
    p = np.arange(128)
    return 16 * (p % 8) + p // 8


def forward_tables():
    y = np.arange(HALF)[:, None]
    tables = []
    for par in range(2):
        lane = np.arange(HALF)[None, :]
        block, slot, t = lane // 128, lane % 128 // 64, lane % 64
        ky = 128 * block + 2 * t + par
        angle = 2 * np.pi * ((ky * y) % NG) / NG
        table = np.where(slot == 0, np.cos(angle), -np.sin(angle))
        if par == 0:
            table[:, 64] = np.where(np.arange(HALF) % 2 == 0, 1.0, -1.0)
        tables.append(np.stack(split_np(table / math.sqrt(NG))))
    return np.stack(tables)


def derivative_table():
    k = np.arange(NG)
    wave = np.where(k < HALF, k, k - NG) * 2 * np.pi / NG
    wave[HALF] = 0.0
    local = row_places()
    target = local
    source = (128 * np.arange(16)[:, None] + local[None, :]).reshape(-1)
    gap = (target[:, None] - source[None, :]) % NG
    rows = [np.real(np.fft.ifft((1j * wave) ** m))[gap] for m in (1, 2, 3)]
    return np.concatenate(split_np(np.concatenate(rows)))


def column_tables():
    k1 = np.arange(128)[:, None]
    i = np.arange(128)[None, :]
    tables = []
    for q in range(16):
        angle = 2 * np.pi * ((q * k1 + 16 * i * k1) % NG) / NG
        c, s = np.cos(angle), np.sin(angle)
        table = np.block([[c, s], [-s, c]]) / math.sqrt(NG)
        tables.append(np.concatenate(split_np(table)))
    return np.stack(tables)


def lane_tables():
    tables = np.zeros((2, 256, 256))
    for par in range(2):
        for t in range(64):
            place = 2 * t + par
            mirrored = (128 - place) % 128
            for slot in range(2):
                source = par * 128 + slot * 64 + t
                tables[0, source, slot * 128 + place] = 1.0
                tables[1, source, slot * 128 + mirrored] = 1.0 - 2.0 * slot
    return tables.astype(ml_dtypes.bfloat16)


def reversal_table():
    table = np.zeros((128, 256))
    table[0, 128] = 1.0
    for k in range(1, 128):
        table[k, 128 - k] = 1.0
    return table.astype(ml_dtypes.bfloat16)


def order_table():
    table = np.zeros((128, 128))
    table[np.arange(128), row_places()] = 1.0
    return table.astype(ml_dtypes.bfloat16)


def split(values):
    hi = values.astype(BF16)
    return hi, (values - hi.astype(F32)).astype(BF16)


def dot(a, b):
    return jnp.dot(a, b, preferred_element_type=F32)


def dot_t(a, b):
    return lax.dot_general(a, b, (((1,), (1,)), ((), ())), preferred_element_type=F32)


def four(a, b, c, d):
    sr, si = a[0] + c[0], a[1] + c[1]
    dr, di = a[0] - c[0], a[1] - c[1]
    tr, ti = b[0] + d[0], b[1] + d[1]
    er, ei = b[0] - d[0], b[1] - d[1]
    return ((sr + tr, si + ti), (dr + ei, di - er), (sr - tr, si - ti), (dr - ei, di + er))


def turned(value, m):
    re, im = value
    if m == 0:
        return value
    if m == 4:
        return (im, -re)
    c, s = math.cos(2 * math.pi * m / 16), math.sin(2 * math.pi * m / 16)
    return (re * c + im * s, im * c - re * s)


def sixteen(values):
    stage = {}
    for q0 in range(4):
        parts = four(*[values[4 * q1 + q0] for q1 in range(4)])
        for ka in range(4):
            stage[ka, q0] = turned(parts[ka], q0 * ka)
    out = [None] * 16
    for ka in range(4):
        parts = four(*[stage[ka, q0] for q0 in range(4)])
        for kb in range(4):
            out[ka + 4 * kb] = parts[kb]
    return out


def waves_of(places):
    signed = jnp.where(places < HALF, places, places - NG)
    signed = jnp.where(places == HALF, 0, signed)
    return signed.astype(F32) * (2.0 * math.pi / NG)


def kernel(
    eta_ref, stress_hbm, wf_hbm, d_hbm, l_hbm, p_ref, j_ref, q_ref, o_ref,
    wf, dm, lm, stress_v, ep, sp, ub, sb1, xr, x2h, x2l, sb2, br,
    ib, fb, sb3, fr, zb, sbuf, slow, fin, ebuf, hr, er, dl, cr, co, cb,
    const_sem, s1, r1, s2, r2, s3, r3, so, ro, se, re_, sc, rc, sd, rd, ls,
):
    tm, space = lax.axis_index("tm"), lax.axis_index("space")
    x, zh, c = space // 4, space // 2 % 2, space % 2
    par = x // 2
    block = (x + par * (3 - 2 * x)) * 4 + zh * 2 + c
    my_r = space
    my_c = par * 8 + block
    my_slice = tm
    is_low = jnp.logical_and(zh == 0, block < 2)
    partner = (tm, (space + 1) % 16)

    def r_dev(s):
        return (tm, s)

    def c_dev(k):
        kp, kb = k // 8, k % 8
        xb = kb // 4
        return (tm, (xb + kp * (3 - 2 * xb)) * 4 + kb % 4)

    def chain_dev(t):
        return (t, space)

    def remote(src, dst, ss, rs, dev):
        return pltpu.make_async_remote_copy(
            src_ref=src, dst_ref=dst, send_sem=ss, recv_sem=rs, device_id=dev, device_id_type=MESH
        )

    barrier = pltpu.get_barrier_semaphore()

    def greet(n, carry):
        pl.semaphore_signal(barrier, inc=1, device_id=(tm, (space + n) % 16), device_id_type=MESH)
        pl.semaphore_signal(barrier, inc=1, device_id=((tm + n) % 16, space), device_id_type=MESH)
        return carry

    lax.fori_loop(1, 16, greet, 0)

    wf_copy = pltpu.make_async_copy(wf_hbm, wf, const_sem.at[0])
    d_copy = pltpu.make_async_copy(d_hbm, dm, const_sem.at[1])
    l_copy = pltpu.make_async_copy(l_hbm, lm, const_sem.at[2])
    stress_load = pltpu.make_async_copy(stress_hbm, stress_v, const_sem.at[3])
    wf_copy.start()

    lane = lax.broadcasted_iota(jnp.int32, (8, 128), 1)
    left = lane < 64
    t_lane = lane % 64
    sign = jnp.where(left, -1.0, 1.0)

    def half_turn(values):
        return pltpu.roll(values, 64, 1)

    def reorder(source, target):
        def body(n, carry):
            cols = pl.ds(pl.multiple_of(n * 256, 256), 256)
            values = source(cols)
            hi = values.astype(BF16)
            rest = values - hi.astype(F32)
            mid = rest.astype(BF16)
            last = (rest - mid.astype(F32)).astype(BF16)
            target[:, cols] = dot(q_ref[...], hi) + dot(q_ref[...], mid) + dot(q_ref[...], last)
            return carry

        lax.fori_loop(0, 8, body, 0)

    reorder(lambda cols: eta_ref[0, :, cols], ep)

    def fold_start(n, carry):
        rows = pl.ds(pl.multiple_of(n * 16, 16), 16)
        lo_rows = pl.ds(pl.multiple_of(n * 16 + 128, 16), 16)
        first, second = ep[rows, :HALF], ep[rows, HALF:]
        for parity, values in ((0, first + second), (1, first - second)):
            hi, lo = split(values)
            ub[parity, rows, :] = hi
            ub[parity, lo_rows, :] = lo
        return carry

    lax.fori_loop(0, 8, fold_start, 0)
    wf_copy.wait()
    d_copy.start()
    stress_load.start()
    l_copy.start()
    pl.semaphore_wait(barrier, 30)

    def begin(k, me, make, src, dst, sem):
        @pl.when(k != me)
        def _():
            make.start()

        @pl.when(k == me)
        def _():
            pltpu.make_async_copy(src, dst, sem).start()

    def t1_copy(k):
        return remote(sb1.at[k], xr.at[my_r], s1.at[k], r1.at[my_r], c_dev(k))

    def forward_start(n, carry):
        parity = n // 4
        cols = pl.ds(pl.multiple_of(n % 4 * 256, 256), 256)
        both = dot(ub[parity], wf[parity, 0, :, cols])
        out = both[:128] + both[128:] + dot(ub[parity, :128, :], wf[parity, 1, :, cols])
        for side in range(2):
            k = parity * 8 + n % 4 * 2 + side
            sb1[k] = out[:, side * 128 : side * 128 + 128].reshape(16, 8, 128)
            begin(k, my_c, t1_copy(k), sb1.at[k], xr.at[my_r], ls.at[0])
        return carry

    lax.fori_loop(0, 8, forward_start, 0)

    def wait_all(buffer, sems, me, sem, count, dev):
        def body(s, carry):
            @pl.when(s != me)
            def _():
                remote(buffer.at[s], buffer.at[s], sems.at[s], sems.at[s], dev).wait_recv()

            @pl.when(s == me)
            def _():
                pltpu.make_async_copy(buffer.at[s], buffer.at[s], sem).wait()

            return carry

        lax.fori_loop(0, count, body, 0)

    wait_all(xr, r1, my_r, ls.at[0], 16, partner)

    def spread(n, carry):
        own = xr[n % 16].reshape(128, 128)
        following = xr[(n + 1) % 16].reshape(128, 128)
        hi, lo = split(jnp.concatenate([own, following], axis=1))
        x2h[n] = hi
        x2l[n] = lo
        return carry

    lax.fori_loop(0, 32, spread, 0)
    d_copy.wait()

    def t2_copy(s):
        return remote(sb2.at[s], br.at[my_c], s2.at[s], r2.at[my_c], r_dev(s))

    def derive(n, carry):
        s = (my_r // 2 + n) % 8 * 2
        xh = x2h[pl.ds(s, 16)].reshape(NG, 256)
        xl = x2l[pl.ds(s, 16)].reshape(NG, 256)
        both = dot(dm[...], xh)
        out = both[:384] + both[384:] + dot(dm[:384, :], xl)
        for side in range(2):
            sb2[s + side] = out[:, side * 128 : side * 128 + 128]
        begin(s, my_r, t2_copy(s), sb2.at[s], br.at[my_c], ls.at[1])
        return carry

    lax.fori_loop(0, 8, derive, 0)

    stress_load.wait()
    for f in range(2):
        reorder(lambda cols: stress_v[f, :, cols], sp.at[f])

    l_copy.wait()

    def column_pass(pair):
        def body(q, carry):
            hi, lo = split(jnp.concatenate(pair(q), axis=0))
            both = dot(lm[q], hi)
            zb[q] = both[:256] + both[256:] + dot(lm[q, :256, :], lo)
            return carry

        lax.fori_loop(0, 16, body, 0)

    def sixteen_at(kt):
        rows = pl.ds(pl.multiple_of(kt * 8, 8), 8)
        im_rows = pl.ds(pl.multiple_of(128 + kt * 8, 8), 8)
        return rows, sixteen([(zb[q, rows, :], zb[q, im_rows, :]) for q in range(16)])

    def start_pair(q):
        values = xr[:, q].reshape(128, 128)
        return [values, half_turn(values)]

    column_pass(start_pair)

    def start_rows(kt, carry):
        rows, out = sixteen_at(kt)
        for k0 in range(16):
            sbuf[k0, rows, :] = jnp.where(left, out[k0][0], half_turn(out[k0][1]))
        return carry

    lax.fori_loop(0, 16, start_rows, 0)

    def reversed_rows(buffer, k0):
        hi, lo = split(jnp.concatenate([buffer[15 - k0], buffer[(16 - k0) % 16]], axis=0))
        return dot(j_ref[...], hi) + dot(j_ref[...], lo)

    lanes128 = lax.broadcasted_iota(jnp.int32, (128, 128), 1)
    at_first = lanes128 % 64 == 0
    conj_sign = jnp.where(lanes128 < 64, 1.0, -1.0)
    has_pack = jnp.logical_and(par == 0, block == 0)

    def keep_low(ci, carry):
        slow[ci] = sbuf[ci + ci // 2 * 12]
        return carry

    lax.fori_loop(0, 4, keep_low, 0)

    @pl.when(has_pack)
    def _():
        def body(ci, carry):
            k0 = ci + ci // 2 * 12
            mirrored = reversed_rows(sbuf, k0) * conj_sign
            slow[ci] = jnp.where(at_first, 0.5 * (sbuf[k0] + mirrored), sbuf[k0])
            return carry

        lax.fori_loop(0, 4, body, 0)

    def leave(make, me):
        def body(n, carry):
            @pl.when(2 * n != me)
            def _():
                make(2 * n).wait_send()

            return carry

        lax.fori_loop(0, 8, body, 0)

    def follow(make, me, ends, sem):
        def body(n, carry):
            k = (me // 2 + n) % 8 * 2 + 1
            src, dst = ends(k)
            begin(k, me, make(k), src, dst, sem)
            return carry

        lax.fori_loop(0, 8, body, 0)

    follow(t2_copy, my_r, lambda s: (sb2.at[s], br.at[my_c]), ls.at[1])
    wait_all(br, r2, my_c, ls.at[1], 16, partner)

    def column_waves(kb, kp, rows):
        lanes = lax.broadcasted_iota(jnp.int32, (rows, 128), 1) % 64
        return (128 * kb + 2 * lanes + kp).astype(F32) * (2.0 * math.pi / NG)

    def pack(k, carry):
        kp, kb = k // 8, k % 8
        ky = column_waves(kb, kp, 128)
        lanes = lax.broadcasted_iota(jnp.int32, (128, 128), 1)
        turn = jnp.where(lanes < 64, -ky, ky)
        weight = jnp.where(jnp.logical_and(k == 0, lanes % 64 == 0), 1.0, 2.0)
        x1, x2, x3 = br[k, 0:128, :], br[k, 128:256, :], br[k, 256:384, :]
        own = sb1[k].reshape(128, 128)
        cols = pl.ds(pl.multiple_of(kb * 128, 128), 128)
        fields = (
            x1,
            x3 - ky * ky * x1,
            half_turn(x2 - ky * ky * own) * turn,
            half_turn(own) * turn,
        )
        for f, values in enumerate(fields):
            hi, lo = split(values * weight)
            ib[kp, f * 128 : f * 128 + 128, cols] = hi
            ib[kp, 512 + f * 128 : 640 + f * 128, cols] = lo
        return carry

    lax.fori_loop(0, 16, pack, 0)

    def fluxes(n, carry):
        rows = pl.ds(pl.multiple_of(n * 256, 256), 256)
        sums = []
        for parity in range(2):
            both = dot_t(ib[parity], wf[parity, 0, rows, :])
            sums.append(both[:512] + both[512:] + dot_t(ib[parity, :512, :], wf[parity, 1, rows, :]))
        results = []
        for half in range(2):
            fields = sums[0] + sums[1] if half == 0 else sums[0] - sums[1]
            cols = pl.ds(pl.multiple_of(n * 256 + half * HALF, 256), 256)
            height = 1.0 + ep[:, cols]
            square = height * height
            mobility = square * height * (1.0 / 3.0)
            marangoni = square / ((1.0 + height) * (1.0 + height))
            shear = 0.5 * square
            results.append((
                mobility * fields[128:256] + marangoni * fields[0:128] + shear * sp[0, :, cols],
                mobility * fields[256:384] + marangoni * fields[384:512] + shear * sp[1, :, cols],
            ))
        for f in range(2):
            for parity in range(2):
                values = results[0][f] + results[1][f] if parity == 0 else results[0][f] - results[1][f]
                hi, lo = split(values)
                fb[parity, f * 128 : f * 128 + 128, rows] = hi
                fb[parity, 256 + f * 128 : 384 + f * 128, rows] = lo
        return carry

    lax.fori_loop(0, 4, fluxes, 0)

    def t3_copy(k):
        return remote(sb3.at[k], fr.at[my_r], s3.at[k], r3.at[my_r], c_dev(k))

    def forward_flux(n, carry):
        parity = n % 2
        cols = pl.ds(pl.multiple_of(n // 2 * 256, 256), 256)
        both = dot(fb[parity], wf[parity, 0, :, cols])
        out = both[:256] + both[256:] + dot(fb[parity, :256, :], wf[parity, 1, :, cols])
        for side in range(2):
            k = parity * 8 + n // 2 * 2 + side
            sb3[k] = out[:, side * 128 : side * 128 + 128].reshape(2, 16, 8, 128)
        k = parity * 8 + n // 2 * 2
        begin(k, my_c, t3_copy(k), sb3.at[k], fr.at[my_r], ls.at[2])
        return carry

    lax.fori_loop(0, 8, forward_flux, 0)

    leave(t3_copy, my_c)
    follow(t3_copy, my_c, lambda k: (sb3.at[k], fr.at[my_r]), ls.at[2])
    wait_all(fr, r3, my_r, ls.at[2], 16, partner)
    ky128 = column_waves(block, par, 128)
    turn128 = jnp.where(lanes128 < 64, -ky128, ky128)

    def flux_pair(q):
        first = fr[:, 0, q].reshape(128, 128)
        second = half_turn(fr[:, 1, q].reshape(128, 128)) * turn128
        return [
            jnp.where(lanes128 < 64, first, half_turn(second)),
            jnp.where(lanes128 < 64, half_turn(first), second),
        ]

    column_pass(flux_pair)
    ky8 = column_waves(block, par, 8)

    def flux_rows(kt, carry):
        rows, out = sixteen_at(kt)
        for k0 in range(16):
            places = 128 * k0 + kt * 8 + lax.broadcasted_iota(jnp.int32, (8, 128), 0)
            kx = waves_of(places)
            square = kx * kx + ky8 * ky8
            scale = DT / (1.0 + (DT * STIFF) * square * square)
            diverge = half_turn(out[k0][0]) * jnp.where(left, 1.0, kx) + out[k0][1] * jnp.where(left, -kx, 1.0)
            fin[k0, rows, :] = sbuf[k0, rows, :] - scale * diverge
        return carry

    lax.fori_loop(0, 16, flux_rows, 0)

    @pl.when(has_pack)
    def _():
        def body(k0, carry):
            mirrored = reversed_rows(fin, k0) * conj_sign
            zb[k0, 0:128, :] = jnp.where(at_first, 0.5 * (fin[k0] + mirrored), fin[k0])
            zb[k0, 128:256, :] = half_turn(fin[k0] - mirrored) * (0.5 * conj_sign)
            return carry

        lax.fori_loop(0, 16, body, 0)

        def back(k0, carry):
            fin[k0] = zb[k0, 0:128, :]
            return carry

        lax.fori_loop(0, 16, back, 0)

    home_b = (tm, block)
    home_m = (tm, 15 - block)
    same_home = block == space
    spans = ((2, 12), (0, 2), (14, 2))

    def out_copies(n):
        first, count = spans[n]
        src = fin.at[pl.ds(first, count)]
        dst = hr.at[par, pl.ds(first, count)]
        return (
            remote(src, dst, so.at[n], ro.at[par, n], home_b),
            remote(src, dst, so.at[3 + n], ro.at[par, n], home_m),
            pltpu.make_async_copy(src, dst, ls.at[3 + n]),
        )

    def begin_out(n):
        direct, mirror, local = out_copies(n)
        mirror.start()

        @pl.when(same_home)
        def _():
            local.start()

        @pl.when(jnp.logical_not(same_home))
        def _():
            direct.start()

    def low_block(t):
        ci = t // 4
        return ci, ci + ci // 2 * 12, pl.multiple_of(t % 4 * 32, 32)

    def low_tables(t):
        ci, k0, first = low_block(t)
        places = 128 * k0 + first + lax.broadcasted_iota(jnp.int32, (32, 128), 0)
        kx = waves_of(places)
        ky = column_waves(block, par, 32)
        square = kx * kx + ky * ky
        gain = 1.0 / (1.0 + DT * (square * square * (1.0 / 3.0) - MEAN_MOBILITY * square))
        return gain, places != NG - 256

    def chain_out(t):
        return remote(dl.at[t], cr.at[my_slice], sc.at[t], rc.at[my_slice], chain_dev(t))

    def chain_back(t):
        return remote(co.at[t], cb.at[my_slice], sd.at[t], rd.at[my_slice], chain_dev(t))

    @pl.when(is_low)
    def _():
        def defects(t, carry):
            ci, k0, first = low_block(t)
            gain, keep = low_tables(t)
            gain = jnp.where(my_slice == 0, 0.0, gain)
            rows = pl.ds(first, 32)
            dl[t] = jnp.where(keep, fin[k0, rows, :] - gain * slow[ci, rows, :], 0.0)
            begin(t, my_slice, chain_out(t), dl.at[t], cr.at[my_slice], ls.at[6])
            return carry

        lax.fori_loop(0, 16, defects, 0)

    begin_out(0)

    @pl.when(is_low)
    def _():
        wait_all(cr, rc, my_slice, ls.at[6], 16, partner)
        gain, keep = low_tables(my_slice)

        def advance(t, current):
            current = gain * current + cr[t]
            co[t] = current
            begin(t, my_slice, chain_back(t), co.at[t], cb.at[my_slice], ls.at[7])
            return current

        lax.fori_loop(0, 16, advance, jnp.zeros((32, 128), F32))
        wait_all(cb, rd, my_slice, ls.at[7], 16, partner)

        def merge(t, carry):
            ci, k0, first = low_block(t)
            gain, keep = low_tables(t)
            rows = pl.ds(first, 32)
            fin[k0, rows, :] = jnp.where(keep, cb[t], fin[k0, rows, :])
            return carry

        lax.fori_loop(0, 16, merge, 0)

    begin_out(1)
    begin_out(2)
    extra_home = jnp.where(block == 0, 8, 16 - block)
    extra_copy = remote(ebuf, er, se.at[0], re_.at[0], (tm, extra_home))

    @pl.when(par == 0)
    def _():
        def body(k0, carry):
            tile = jnp.transpose(jnp.where(has_pack, zb[k0, 128:256, :], fin[k0]))
            ebuf[k0, 0:1, :] = tile[0:1, :]
            ebuf[k0, 1:2, :] = tile[64:65, :]
            return carry

        lax.fori_loop(0, 16, body, 0)
        extra_copy.start()


    is_mirror = space >= 8

    def arrived(n):
        first, count = spans[n]
        for source_par in range(2):
            local_here = jnp.logical_and(same_home, par == source_par)
            view = hr.at[source_par, pl.ds(first, count)]

            @pl.when(local_here)
            def _():
                pltpu.make_async_copy(view, view, ls.at[3 + n]).wait()

            @pl.when(jnp.logical_not(local_here))
            def _():
                remote(view, view, ro.at[source_par, n], ro.at[source_par, n], partner).wait_recv()

    def ordered(k0, table):
        hi, lo = split(jnp.concatenate([hr[0, k0], hr[1, k0]], axis=1))
        return dot(hi, table) + dot(lo, table)

    def put(k0, values):
        rows = pl.ds(pl.multiple_of(k0 * 128, 128), 128)
        o_ref[0, 0, rows, :] = values[:, :128]
        o_ref[0, 1, rows, :] = values[:, 128:]

    def order_span(n):
        first, count = spans[n]

        @pl.when(jnp.logical_not(is_mirror))
        def _():
            def body(k0, carry):
                put(k0, ordered(k0, p_ref[0]))
                return carry

            lax.fori_loop(first, first + count, body, 0)

        @pl.when(is_mirror)
        def _():
            def body(k0, carry):
                values = ordered(k0, p_ref[1])
                zb[k0, 0:128, :] = values[:, :128]
                zb[k0, 128:256, :] = values[:, 128:]
                return carry

            lax.fori_loop(first, first + count, body, 0)

    def turn_rows(k0, carry):
        one, two = 15 - k0, (16 - k0) % 16
        upper = jnp.concatenate([zb[one, 0:128, :], zb[one, 128:256, :]], axis=1)
        lower = jnp.concatenate([zb[two, 0:128, :], zb[two, 128:256, :]], axis=1)
        hi, lo = split(jnp.concatenate([upper, lower], axis=0))
        put(k0, dot(j_ref[...], hi) + dot(j_ref[...], lo))
        return carry

    arrived(0)
    order_span(0)

    @pl.when(is_mirror)
    def _():
        lax.fori_loop(3, 14, turn_rows, 0)

    for n in (1, 2):
        arrived(n)
        order_span(n)

    @pl.when(is_mirror)
    def _():
        lax.fori_loop(0, 3, turn_rows, 0)
        lax.fori_loop(14, 16, turn_rows, 0)
        remote(er, er, re_.at[0], re_.at[0], partner).wait_recv()

        def patch(k0, carry):
            both = jnp.concatenate([er[15 - k0], er[(16 - k0) % 16]], axis=1)
            hi, lo = split(jnp.concatenate([both, both], axis=0))
            turned_rows = dot_t(hi, j_ref[...]) + dot_t(lo, j_ref[...])
            rows = lax.broadcasted_iota(jnp.int32, (128, 128), 0)
            tile = jnp.where(
                rows == 0, turned_rows[0:1, :], jnp.where(rows == 64, turned_rows[1:2, :], 0.0)
            )
            extra = jnp.transpose(tile)
            place = pl.ds(pl.multiple_of(k0 * 128, 128), 128)
            o_ref[0, 0, place, :] = jnp.where(lanes128 == 0, extra, o_ref[0, 0, place, :])
            o_ref[0, 1, place, :] = jnp.where(lanes128 == 0, -half_turn(extra), o_ref[0, 1, place, :])
            return carry

        lax.fori_loop(0, 16, patch, 0)

    def sent(k, carry):
        @pl.when(k != my_c)
        def _():
            t1_copy(k).wait_send()

        @pl.when(jnp.logical_and(k % 2 == 1, k != my_c))
        def _():
            t3_copy(k).wait_send()

        @pl.when(k != my_r)
        def _():
            t2_copy(k).wait_send()

        return carry

    lax.fori_loop(0, 16, sent, 0)
    for n in range(3):
        direct, mirror, local = out_copies(n)
        mirror.wait_send()

        @pl.when(jnp.logical_not(same_home))
        def _():
            direct.wait_send()

    @pl.when(par == 0)
    def _():
        extra_copy.wait_send()

    @pl.when(is_low)
    def _():
        def body(t, carry):
            @pl.when(t != my_slice)
            def _():
                chain_out(t).wait_send()
                chain_back(t).wait_send()

            return carry

        lax.fori_loop(0, 16, body, 0)


def solution(mesh):
    tables = [
        forward_tables(),
        derivative_table(),
        column_tables(),
        lane_tables(),
        reversal_table(),
        order_table(),
    ]
    vmem = pl.BlockSpec(memory_space=pltpu.VMEM)
    anywhere = pl.BlockSpec(memory_space=pl.ANY)
    dma = pltpu.SemaphoreType.DMA

    def shards(starts, stress):
        return pl.pallas_call(
            kernel,
            out_shape=jax.ShapeDtypeStruct((1, 2, NG, 128), F32),
            in_specs=[vmem, anywhere, anywhere, anywhere, anywhere, vmem, vmem, vmem],
            out_specs=vmem,
            scratch_shapes=[
                pltpu.VMEM((2, 2, HALF, HALF), BF16),
                pltpu.VMEM((768, NG), BF16),
                pltpu.VMEM((16, 512, 256), BF16),
                pltpu.VMEM((2, 128, NG), F32),
                pltpu.VMEM((128, NG), F32),
                pltpu.VMEM((2, 128, NG), F32),
                pltpu.VMEM((2, 256, HALF), BF16),
                pltpu.VMEM((16, 16, 8, 128), F32),
                pltpu.VMEM((16, 16, 8, 128), F32),
                pltpu.VMEM((32, 128, 256), BF16),
                pltpu.VMEM((32, 128, 256), BF16),
                pltpu.VMEM((16, 384, 128), F32),
                pltpu.VMEM((16, 384, 128), F32),
                pltpu.VMEM((2, 1024, HALF), BF16),
                pltpu.VMEM((2, 512, HALF), BF16),
                pltpu.VMEM((16, 2, 16, 8, 128), F32),
                pltpu.VMEM((16, 2, 16, 8, 128), F32),
                pltpu.VMEM((16, 256, 128), F32),
                pltpu.VMEM((16, 128, 128), F32),
                pltpu.VMEM((4, 128, 128), F32),
                pltpu.VMEM((16, 128, 128), F32),
                pltpu.VMEM((16, 8, 128), F32),
                pltpu.VMEM((2, 16, 128, 128), F32),
                pltpu.VMEM((16, 8, 128), F32),
                pltpu.VMEM((16, 32, 128), F32),
                pltpu.VMEM((16, 32, 128), F32),
                pltpu.VMEM((16, 32, 128), F32),
                pltpu.VMEM((16, 32, 128), F32),
                dma((4,)),
                dma((16,)), dma((16,)), dma((16,)), dma((16,)), dma((16,)), dma((16,)),
                dma((6,)), dma((2, 3)), dma((1,)), dma((1,)),
                dma((16,)), dma((16,)), dma((16,)), dma((16,)), dma((8,)),
            ],
            compiler_params=pltpu.CompilerParams(
                collective_id=0, has_side_effects=True, vmem_limit_bytes=62 * 1024 * 1024
            ),
            name="parareal",
        )(starts, stress, *[jnp.asarray(table) for table in tables])

    return jax.shard_map(
        shards,
        mesh=mesh,
        in_specs=(P("tm", "space", None), P(None, "space", None)),
        out_specs=P("tm", None, None, "space"),
        check_vma=False,
    )
```
